32 devices in a mesh: parts: 2 (over x), tm: 2 (over core), pix: 8 (over z, y).
Axes of the slice: x: 2, y: 2, z: 4, core: 2. Of those that a mesh axis runs over, the one named last changes fastest.
Arguments:
- frames: bfloat16 [64, 256, 2048], P(('parts', 'tm', 'pix')), parts along dimension 0, may hold values from 2.2 to 19
- dark: bfloat16 [8, 256, 2048], P('parts', None, 'pix'), parts along dimension 0, may hold values from 0 to 2
- dark_index: int32 [64], P(('parts', 'tm')), parts along dimension 0, may hold values from 0 to 3
- cycle_counts: int32 [256], replicated, may hold values from 1024 to 2048, as said below
Outputs:
- correlation: float32 [256, 64, 32], P('pix', ('parts', 'tm')), parts along dimension 1
The draws below stay inside these ranges and needn't reach their ends.
There are 2 independent parts, one for each index of `parts`. The reference program is written for one: setup_inputs(seed, part) draws one part's arguments, and reference() takes and returns one part's arrays. A program takes and returns all parts, laid end to end along the dimension named above; an argument that names none is the same for every part. Nothing has to cross between parts.
Inputs may be any that keep to these rules, and one draw needn't show every extreme that they name: `cycle_counts`: at least one cycle has all 2048 slots live and at least one has exactly half of them.
All inputs are finite; a program needn't handle non-finite values.
Results may differ from the reference program's by a relative error of at most 0.0003.
Values may be sent and summed in bfloat16 or wider, within the bound.
No kernel may reach another device: no remote copies, remote signals or barrier semaphores. Data moves between devices by JAX's collectives and lax.ppermute only.
A program may use at most 128 MiB of HBM per device.

```python
import math
import jax
import jax.numpy as jnp
from jax import lax

Q = 256
ND = 4
PR = 2048
F = 32


def draw_frames(key, part):
    key_rate, key_freq, key_phase, key_bright, key_shot, key_flux = jax.random.split(key, 6)
    frame_pos = jnp.arange(F, dtype=jnp.float32)
    aging_rate = 0.5
    brightness = jax.random.uniform(key_bright, (Q, PR), jnp.float32, 0.5, 3.0)
    beam_flux = jax.random.uniform(key_flux, (F,), jnp.float32, 0.7, 1.3)
    decay_rate = jnp.exp(jax.random.uniform(key_rate, (Q,), jnp.float32, math.log(2.0 / F), math.log(0.3)))
    frequency = decay_rate[None, :, None] * jax.random.normal(key_freq, (3, Q, PR), jnp.float32)
    phases = jax.random.uniform(key_phase, (3, Q, PR), jnp.float32, -math.pi, math.pi)
    frame_clock = frame_pos + aging_rate * frame_pos * frame_pos / F
    beating = jnp.zeros((F, Q, PR), jnp.float32)
    for first_mode, second_mode in ((0, 1), (0, 2), (1, 2)):
        pair_freq = frequency[first_mode] - frequency[second_mode]
        pair_phase = phases[first_mode] - phases[second_mode]
        beating = beating + jnp.cos(pair_freq[None] * frame_clock[:, None, None] + pair_phase[None])
    speckle = 1.0 + 2.0 / 3.0 * beating
    shot_noise = jax.random.uniform(key_shot, (F, Q, PR), jnp.float32, 0.75, 1.25)
    intensity = beam_flux[:, None, None] * (3.2 + brightness[None] * speckle * shot_noise)
    return intensity.astype(jnp.bfloat16)


def draw_dark(key, part):
    key_level, key_pattern = jax.random.split(key)
    offsets = jax.random.uniform(key_level, (ND,), jnp.float32)
    levels = 1.6 * (jnp.arange(ND, dtype=jnp.float32) + offsets) / ND
    pattern = jax.random.uniform(key_pattern, (ND, Q, PR), jnp.float32, 0.0, 0.4)
    return (levels[:, None, None] + pattern).astype(jnp.bfloat16)


def draw_cycle_counts(key, part):
    key_counts, key_pick = jax.random.split(key)
    base_counts = jax.random.randint(key_counts, (Q,), PR // 2, PR + 1, dtype=jnp.int32)
    picked = jax.random.permutation(key_pick, Q).astype(jnp.int32)
    cycle_ids = jnp.arange(Q, dtype=jnp.int32)
    with_full = jnp.where(cycle_ids == picked[0], PR, base_counts)
    return jnp.where(cycle_ids == picked[1], PR // 2, with_full).astype(jnp.int32)


def place_ends(values, stream_key, smallest, high):
    place = [jax.random.randint(jax.random.fold_in(stream_key, axis), (), 0, length) for axis, length in enumerate(values.shape)]
    longest = values.shape.index(max(values.shape))
    next_to = place[:longest] + [(place[longest] + 1) % values.shape[longest]] + place[longest + 1:]
    return values.at[tuple(place)].set(smallest).at[tuple(next_to)].set(high)


def setup_inputs(seed: int = 0, part: int = 0) -> dict:
    key_list = jax.random.split(jax.random.key(seed), 5)
    part_keys = jax.random.split(jax.random.fold_in(key_list[4], part), 5)
    frames = draw_frames(jax.random.fold_in(jax.random.fold_in(key_list[4], part), 71), part)
    dark = draw_dark(jax.random.fold_in(jax.random.fold_in(key_list[4], part), 71), part)
    dark_index = place_ends(jax.random.randint(part_keys[2], (F,), 0, ND), jax.random.fold_in(part_keys[2], 1), 0, ND - 1).astype(jnp.int32)
    cycle_counts = draw_cycle_counts(jax.random.fold_in(key_list[4], 71), part)
    return dict(frames=frames, dark=dark, dark_index=dark_index, cycle_counts=cycle_counts)


cycles_per_block = 8


def reference(frames, dark, dark_index, cycle_counts):
    slot_index = jnp.arange(PR, dtype=jnp.int32)

    def cycle_block_corr(first_cycle):
        raw_block = lax.dynamic_slice_in_dim(frames, first_cycle, cycles_per_block, 1).astype(jnp.float32)
        dark_block = lax.dynamic_slice_in_dim(dark, first_cycle, cycles_per_block, 1).astype(jnp.float32)[dark_index]
        block_counts = lax.dynamic_slice_in_dim(cycle_counts, first_cycle, cycles_per_block, 0)
        live_slot = slot_index[None, :] < block_counts[:, None]
        corrected = jnp.where(live_slot[None], raw_block - dark_block, jnp.float32(0.0)).astype(jnp.bfloat16)
        signal = lax.optimization_barrier(corrected).astype(jnp.float32)
        gram_sum = jnp.einsum("tqs,uqs->qtu", signal, signal, precision=lax.Precision.HIGHEST)
        cycle_sums = jnp.sum(signal, axis=2).T
        live_counts = block_counts.astype(jnp.float32)
        return gram_sum * live_counts[:, None, None] / (cycle_sums[:, :, None] * cycle_sums[:, None, :])

    result = lax.map(cycle_block_corr, jnp.arange(0, Q, cycles_per_block, dtype=jnp.int32))
    return result.reshape(Q, F, F)
```

```python
import functools

import jax
import jax.numpy as jnp
import numpy as np
from jax import lax
from jax.experimental import pallas as pl
from jax.experimental.pallas import tpu as pltpu
from jax.sharding import PartitionSpec as P

LANES = 128
ROWS = 16
VMEM_LIMIT = 48 * 1024 * 1024


def subtract_dark(raw_frames, dark_frames, dark_index, live_slot):
    values = raw_frames.astype(jnp.float32)
    for dark_level in range(dark_frames.shape[0]):
        picked = (dark_index == dark_level)[:, None, None]
        values = values - jnp.where(
            picked, dark_frames[dark_level].astype(jnp.float32)[None], jnp.float32(0.0)
        )
    return jnp.where(live_slot[None], values, jnp.float32(0.0)).astype(jnp.bfloat16)


def correlate(row_signal, col_signal):
    gram_tiles = jnp.einsum(
        "tqs,uqs->qtu", row_signal, col_signal, preferred_element_type=jnp.float32
    )
    totals = jnp.sum(col_signal, axis=2, dtype=jnp.float32).T
    return (gram_tiles, totals)


def plain_local(frames, dark, dark_index, cycle_counts):
    pix_count = lax.axis_size("pix")
    pix_index = lax.axis_index("pix")
    tm_index = lax.axis_index("tm")
    owned_cycles = frames.shape[1] // pix_count
    regrouped = lax.all_to_all(frames, "pix", split_axis=1, concat_axis=0, tiled=True)
    dark_cycles = lax.all_to_all(dark, "pix", split_axis=1, concat_axis=2, tiled=True)
    block_counts = lax.dynamic_slice_in_dim(cycle_counts, pix_index * owned_cycles, owned_cycles, 0)
    live_slot = jnp.arange(regrouped.shape[2], dtype=jnp.int32)[None, :] < block_counts[:, None]
    signal = subtract_dark(regrouped, dark_cycles, dark_index, live_slot)
    half_frames = signal.shape[0]
    all_frames = lax.all_gather(signal, "tm", axis=0, tiled=True)
    gram_tiles, totals = correlate(signal, all_frames)
    live_counts = lax.dynamic_slice_in_dim(
        cycle_counts, pix_index * owned_cycles, owned_cycles, 0
    ).astype(jnp.float32)
    row_totals = lax.dynamic_slice_in_dim(totals, tm_index * half_frames, half_frames, 1)
    return gram_tiles * live_counts[:, None, None] / (row_totals[:, :, None] * totals[:, None, :])


def pack_kernel(n_pix, place, frames, other, dark, *outs):
    per_device, slots = frames.shape[0], frames.shape[-1]
    tiles = slots // LANES
    for k in range(n_pix):
        dest = place[0] ^ k
        row = 0
        for f in range(2 * per_device):
            for j in range(tiles):
                lanes = pl.ds(j * LANES, LANES)
                if f < per_device:
                    block = frames[f, dest, 0, :, lanes]
                else:
                    block = other[f - per_device, dest, :, lanes]
                outs[k][pl.ds(row, ROWS), :] = block
                row += ROWS
        for level in range(dark.shape[0]):
            for j in range(dark.shape[-1] // LANES):
                outs[k][pl.ds(row, ROWS), :] = dark[level, dest, 0, :, pl.ds(j * LANES, LANES)]
                row += ROWS


def split3(x):
    high = x.astype(jnp.bfloat16)
    rest = x - high.astype(jnp.float32)
    middle = rest.astype(jnp.bfloat16)
    low = (rest - middle.astype(jnp.float32)).astype(jnp.bfloat16)
    return high, middle, low


def pick(x, chosen):
    return sum(jnp.dot(part, chosen, preferred_element_type=jnp.float32) for part in split3(x))


def gram_kernel(n_pix, per_device, levels, place, own_index, other_index, counts_col, counts_row, repeat, reorder, *refs):
    bufs, (out, signal, dark) = refs[:n_pix], refs[n_pix:]
    me, core = place[0], place[1]
    frames_half = per_device * n_pix
    n_frames = 2 * frames_half
    slots = signal.shape[1]
    tiles = slots // LANES
    dark_tiles = tiles // n_pix
    dark_row = 2 * per_device * tiles * ROWS
    counts = counts_col[...]
    lane = lax.broadcasted_iota(jnp.int32, (ROWS, LANES), 1)
    live = [lane + j * LANES < counts for j in range(tiles)]
    for k in range(n_pix):
        source = me ^ k
        for j in range(dark_tiles):
            for level in range(levels):
                row = dark_row + (level * dark_tiles + j) * ROWS
                dark[source * dark_tiles + j, pl.ds(level * ROWS, ROWS), :] = bufs[k][
                    pl.ds(row, ROWS), :
                ].astype(jnp.float32)
    for k in range(n_pix):
        source = me ^ k
        for f in range(2 * per_device):
            local_frame = source * per_device + f % per_device
            if f < per_device:
                level, half = own_index[local_frame], core
            else:
                level, half = other_index[local_frame], 1 - core
            first = pl.multiple_of((half * frames_half + local_frame) * ROWS, ROWS)
            dark_first = pl.multiple_of(level * ROWS, ROWS)
            for j in range(tiles):
                raw = bufs[k][pl.ds((f * tiles + j) * ROWS, ROWS), :].astype(jnp.float32)
                value = raw - dark[j, pl.ds(dark_first, ROWS), :]
                value = jnp.where(live[j], value, 0.0)
                signal[pl.ds(first, ROWS), pl.ds(j * LANES, LANES)] = value.astype(jnp.bfloat16)
    contract = (((1,), (1,)), ((), ()))
    width = n_frames * ROWS
    every = signal[...]
    totals = lax.dot_general(
        jnp.ones((ROWS, slots), jnp.bfloat16), every, contract, preferred_element_type=jnp.float32
    )
    same = (
        lax.broadcasted_iota(jnp.int32, (ROWS, width), 0)
        == lax.broadcasted_iota(jnp.int32, (ROWS, width), 1) % ROWS
    )
    diagonal = []
    step = 8
    for block in range(n_frames // step):
        part = lax.dot_general(
            signal[pl.ds(block * step * ROWS, step * ROWS), :], every, contract,
            preferred_element_type=jnp.float32,
        ).reshape(step, ROWS, width)
        diagonal.append(jnp.sum(jnp.where(same[None], part, 0.0), axis=1))
    gram = jnp.concatenate(diagonal, axis=0)
    mine = (
        lax.broadcasted_iota(jnp.int32, (n_frames, width), 0)
        == lax.broadcasted_iota(jnp.int32, (n_frames, width), 1) // ROWS
    )
    col_totals = totals[0:1, :]
    row_totals = pick(jnp.where(mine, col_totals, 0.0), repeat[...])
    ratio = gram * counts_row[...] / (row_totals * col_totals)
    ordered = pick(ratio, reorder[...])
    for q in range(ROWS):
        out[q] = ordered[:, q * n_frames : (q + 1) * n_frames]


def in_vmem(count):
    return [pl.BlockSpec(memory_space=pltpu.VMEM)] * count


def in_smem(count):
    return [pl.BlockSpec(memory_space=pltpu.SMEM)] * count


def packed_local(frames, dark, dark_index, cycle_counts):
    n_pix, core, me = lax.axis_size("pix"), lax.axis_index("tm"), lax.axis_index("pix")
    per_device, _, slots = frames.shape
    levels, _, dark_slots = dark.shape
    n_frames = 2 * per_device * n_pix
    swap = [(0, 1), (1, 0)]
    split_frames = frames.reshape(per_device, n_pix, 2, ROWS, slots)
    split_dark = dark.reshape(levels, n_pix, 2, ROWS, dark_slots)
    place = jnp.stack([me, core]).astype(jnp.int32)
    other = lax.ppermute(
        lax.dynamic_index_in_dim(split_frames, 1 - core, 2, keepdims=False), "tm", swap
    )
    other_index = lax.ppermute(dark_index, "tm", swap)
    own_frames = lax.dynamic_slice_in_dim(split_frames, core, 1, 2)
    own_dark = lax.dynamic_slice_in_dim(split_dark, core, 1, 2)
    rows = (2 * per_device * slots + levels * dark_slots) // LANES * ROWS
    packed = pl.pallas_call(
        functools.partial(pack_kernel, n_pix),
        out_shape=[jax.ShapeDtypeStruct((rows, LANES), frames.dtype)] * n_pix,
        in_specs=in_smem(1) + in_vmem(3),
        out_specs=in_vmem(n_pix),
        compiler_params=pltpu.CompilerParams(vmem_limit_bytes=VMEM_LIMIT),
        name="pack",
    )(place, own_frames, other, own_dark)
    received = [packed[0]] + [None] * (n_pix - 1)
    half = n_pix // 2
    order = [k for pair in zip(range(half, n_pix), range(1, half + 1)) for k in pair if k != half or pair[0] == half]
    order = list(dict.fromkeys(order))
    for k in order:
        received[k] = lax.ppermute(packed[k], "pix", [(i, i ^ k) for i in range(n_pix)])
    counts = lax.dynamic_slice_in_dim(cycle_counts, (2 * me + core) * ROWS, ROWS, 0)
    width = n_frames * ROWS
    counts_col = jnp.broadcast_to(counts[:, None], (ROWS, LANES))
    counts_row = jnp.tile(counts.astype(jnp.float32), n_frames)[None]
    index = np.arange(width)
    cycle, frame = index % ROWS, index // ROWS
    repeat = jnp.asarray(cycle[:, None] == cycle[None, :], jnp.bfloat16)
    reorder = jnp.asarray((cycle * n_frames + frame)[:, None] == index[None, :], jnp.bfloat16)
    blocks = pl.pallas_call(
        functools.partial(gram_kernel, n_pix, per_device, levels),
        out_shape=jax.ShapeDtypeStruct((ROWS, n_frames, n_frames), jnp.float32),
        in_specs=in_smem(3) + in_vmem(4 + n_pix),
        out_specs=in_vmem(1)[0],
        scratch_shapes=[
            pltpu.VMEM((width, slots), jnp.bfloat16),
            pltpu.VMEM((slots // LANES, levels * ROWS, LANES), jnp.float32),
        ],
        compiler_params=pltpu.CompilerParams(vmem_limit_bytes=VMEM_LIMIT),
        name="gram",
    )(place, dark_index, other_index, counts_col, counts_row, repeat, reorder, *received)
    n_half = n_frames // 2
    mine = lax.dynamic_slice_in_dim(blocks, core * n_half, n_half, 1)
    theirs = lax.ppermute(
        lax.dynamic_slice_in_dim(blocks, (1 - core) * n_half, n_half, 1), "tm", swap
    )
    lower = core == 0
    return jnp.concatenate(
        [jnp.where(lower, mine, theirs), jnp.where(lower, theirs, mine)], axis=0
    )


def solution(mesh):
    n_pix, n_tm = mesh.shape["pix"], mesh.shape["tm"]

    def local(frames, dark, dark_index, cycle_counts):
        owned, slots = frames.shape[1] // n_pix, frames.shape[2]
        fits = n_tm == 2 and owned == 2 * ROWS and n_pix & (n_pix - 1) == 0 and n_pix <= 8
        fits = fits and dark.shape[2] % LANES == 0 and slots == dark.shape[2] * n_pix
        return (packed_local if fits else plain_local)(frames, dark, dark_index, cycle_counts)

    in_specs = (
        P(("parts", "tm", "pix"), None, None),
        P("parts", None, "pix"),
        P(("parts", "tm")),
        P(),
    )
    out_specs = P("pix", ("parts", "tm"), None)
    return jax.shard_map(local, mesh=mesh, in_specs=in_specs, out_specs=out_specs, check_vma=False)
```

```python
import functools

import jax
import jax.numpy as jnp
import numpy as np
from jax import lax
from jax.experimental import pallas as pl
from jax.experimental.pallas import tpu as pltpu
from jax.sharding import PartitionSpec as P

LANES = 128
ROWS = 16
FIRST = 2
VMEM_LIMIT = 48 * 1024 * 1024


def subtract_dark(raw_frames, dark_frames, dark_index, live_slot):
    values = raw_frames.astype(jnp.float32)
    for dark_level in range(dark_frames.shape[0]):
        picked = (dark_index == dark_level)[:, None, None]
        values = values - jnp.where(
            picked, dark_frames[dark_level].astype(jnp.float32)[None], jnp.float32(0.0)
        )
    return jnp.where(live_slot[None], values, jnp.float32(0.0)).astype(jnp.bfloat16)


def correlate(row_signal, col_signal):
    gram_tiles = jnp.einsum(
        "tqs,uqs->qtu", row_signal, col_signal, preferred_element_type=jnp.float32
    )
    totals = jnp.sum(col_signal, axis=2, dtype=jnp.float32).T
    return (gram_tiles, totals)


def plain_local(frames, dark, dark_index, cycle_counts):
    pix_count = lax.axis_size("pix")
    pix_index = lax.axis_index("pix")
    tm_index = lax.axis_index("tm")
    owned_cycles = frames.shape[1] // pix_count
    regrouped = lax.all_to_all(frames, "pix", split_axis=1, concat_axis=0, tiled=True)
    dark_cycles = lax.all_to_all(dark, "pix", split_axis=1, concat_axis=2, tiled=True)
    block_counts = lax.dynamic_slice_in_dim(cycle_counts, pix_index * owned_cycles, owned_cycles, 0)
    live_slot = jnp.arange(regrouped.shape[2], dtype=jnp.int32)[None, :] < block_counts[:, None]
    signal = subtract_dark(regrouped, dark_cycles, dark_index, live_slot)
    half_frames = signal.shape[0]
    all_frames = lax.all_gather(signal, "tm", axis=0, tiled=True)
    gram_tiles, totals = correlate(signal, all_frames)
    live_counts = lax.dynamic_slice_in_dim(
        cycle_counts, pix_index * owned_cycles, owned_cycles, 0
    ).astype(jnp.float32)
    row_totals = lax.dynamic_slice_in_dim(totals, tm_index * half_frames, half_frames, 1)
    return gram_tiles * live_counts[:, None, None] / (row_totals[:, :, None] * totals[:, None, :])


def pack_kernel(n_pix, messages, place, frames, dark, *refs):
    count = len(messages)
    outs, (raw, shade, raw_sem, shade_sem) = refs[:count], refs[count:]
    per_device, slots = frames.shape[0], frames.shape[-1]
    share = shade.shape[1]
    copies = []
    for n, k in enumerate(messages):
        dest, half = place[0] ^ (k % n_pix), place[1] ^ (k // n_pix)
        copies.append((
            pltpu.make_async_copy(frames.at[:, dest, half], raw.at[n], raw_sem.at[n]),
            pltpu.make_async_copy(
                dark.at[pl.ds(place[1] * share, share), dest, half], shade.at[n], shade_sem.at[n]
            ),
        ))
        for copy in copies[-1]:
            copy.start()
    for n in range(count):
        for copy in copies[n]:
            copy.wait()
        row = 0
        for block, depth in ((raw, per_device), (shade, share)):
            for f in range(depth):
                for j in range(block.shape[-1] // LANES):
                    outs[n][pl.ds(row, ROWS), :] = block[n, f, :, pl.ds(j * LANES, LANES)]
                    row += ROWS


def split3(x):
    high = x.astype(jnp.bfloat16)
    rest = x - high.astype(jnp.float32)
    middle = rest.astype(jnp.bfloat16)
    low = (rest - middle.astype(jnp.float32)).astype(jnp.bfloat16)
    return high, middle, low


def pick(x, chosen):
    return sum(jnp.dot(part, chosen, preferred_element_type=jnp.float32) for part in split3(x))


def gram_kernel(n_pix, per_device, levels, place, own_index, other_index, counts_col, counts_row, repeat, reorder, *refs):
    n_bufs = 2 * n_pix
    bufs, (out, signal, dark) = refs[:n_bufs], refs[n_bufs:]
    me, core = place[0], place[1]
    share = levels // 2
    frames_half = per_device * n_pix
    n_frames = 2 * frames_half
    slots = signal.shape[1]
    tiles = slots // LANES
    dark_tiles = tiles // n_pix
    dark_row = per_device * tiles * ROWS
    counts = counts_col[...]
    lane = lax.broadcasted_iota(jnp.int32, (ROWS, LANES), 1)
    live = [lane + j * LANES < counts for j in range(tiles)]
    for k in range(n_bufs):
        source, half = me ^ (k % n_pix), core ^ (k // n_pix)
        for j in range(dark_tiles):
            for n in range(share):
                level = pl.multiple_of((half * share + n) * ROWS, ROWS)
                row = dark_row + (n * dark_tiles + j) * ROWS
                dark[source * dark_tiles + j, pl.ds(level, ROWS), :] = bufs[k][
                    pl.ds(row, ROWS), :
                ].astype(jnp.float32)
    for k in range(n_bufs):
        source, half = me ^ (k % n_pix), core ^ (k // n_pix)
        index = own_index if k < n_pix else other_index
        for f in range(per_device):
            frame = source * per_device + f
            first = pl.multiple_of((half * frames_half + frame) * ROWS, ROWS)
            dark_first = pl.multiple_of(index[frame] * ROWS, ROWS)
            for j in range(tiles):
                raw = bufs[k][pl.ds((f * tiles + j) * ROWS, ROWS), :].astype(jnp.float32)
                value = raw - dark[j, pl.ds(dark_first, ROWS), :]
                value = jnp.where(live[j], value, 0.0)
                signal[pl.ds(first, ROWS), pl.ds(j * LANES, LANES)] = value.astype(jnp.bfloat16)
    contract = (((1,), (1,)), ((), ()))
    width = n_frames * ROWS
    every = signal[...]
    totals = lax.dot_general(
        jnp.ones((ROWS, slots), jnp.bfloat16), every, contract, preferred_element_type=jnp.float32
    )
    same = (
        lax.broadcasted_iota(jnp.int32, (ROWS, width), 0)
        == lax.broadcasted_iota(jnp.int32, (ROWS, width), 1) % ROWS
    )
    products = lax.dot_general(every, every, contract, preferred_element_type=jnp.float32)
    products = products.reshape(n_frames, ROWS, width)
    gram = jnp.sum(jnp.where(same[None], products, 0.0), axis=1)
    mine = (
        lax.broadcasted_iota(jnp.int32, (n_frames, width), 0)
        == lax.broadcasted_iota(jnp.int32, (n_frames, width), 1) // ROWS
    )
    col_totals = totals[0:1, :]
    row_totals = pick(jnp.where(mine, col_totals, 0.0), repeat[...])
    ratio = gram * counts_row[...] / (row_totals * col_totals)
    ordered = pick(ratio, reorder[...])
    for q in range(ROWS):
        out[q] = ordered[:, q * n_frames : (q + 1) * n_frames]


def in_vmem(count):
    return [pl.BlockSpec(memory_space=pltpu.VMEM)] * count


def in_smem(count):
    return [pl.BlockSpec(memory_space=pltpu.SMEM)] * count


def packed_local(frames, dark, dark_index, cycle_counts):
    n_pix, core, me = lax.axis_size("pix"), lax.axis_index("tm"), lax.axis_index("pix")
    per_device, _, slots = frames.shape
    levels, _, dark_slots = dark.shape
    n_frames = 2 * per_device * n_pix
    swap = [(0, 1), (1, 0)]
    split_frames = frames.reshape(per_device, n_pix, 2, ROWS, slots)
    split_dark = dark.reshape(levels, n_pix, 2, ROWS, dark_slots)
    share = levels // 2
    place = jnp.stack([me, core]).astype(jnp.int32)
    rows = (per_device * slots + share * dark_slots) // LANES * ROWS
    half = n_pix // 2
    far = [t * n_pix + k for t in range(2) for k in range(half, n_pix)]
    near = [t * n_pix + k for t in range(2) for k in range(1, half)] + [n_pix]
    order = [k for pair in zip(far, near) for k in pair] + far[len(near) :]
    packed = {}
    for messages in (order[:FIRST], order[FIRST:] + [0]):
        count = len(messages)
        buffers = pl.pallas_call(
            functools.partial(pack_kernel, n_pix, messages),
            out_shape=[jax.ShapeDtypeStruct((rows, LANES), frames.dtype)] * count,
            in_specs=in_smem(1) + [pl.BlockSpec(memory_space=pl.ANY)] * 2,
            out_specs=in_vmem(count),
            scratch_shapes=[
                pltpu.VMEM((count, per_device, ROWS, slots), frames.dtype),
                pltpu.VMEM((count, share, ROWS, dark_slots), dark.dtype),
                pltpu.SemaphoreType.DMA((count,)),
                pltpu.SemaphoreType.DMA((count,)),
            ],
            compiler_params=pltpu.CompilerParams(vmem_limit_bytes=VMEM_LIMIT),
            name="pack",
        )(place, split_frames, split_dark)
        packed.update(zip(messages, buffers))
    received = [packed[0]] + [None] * (2 * n_pix - 1)
    for k in order:
        received[k] = lax.ppermute(
            packed[k], ("tm", "pix"), [(i, i ^ k) for i in range(2 * n_pix)]
        )
    other_index = lax.ppermute(dark_index, "tm", swap)
    counts = lax.dynamic_slice_in_dim(cycle_counts, (2 * me + core) * ROWS, ROWS, 0)
    width = n_frames * ROWS
    counts_col = jnp.broadcast_to(counts[:, None], (ROWS, LANES))
    counts_row = jnp.tile(counts.astype(jnp.float32), n_frames)[None]
    index = np.arange(width)
    cycle, frame = index % ROWS, index // ROWS
    repeat = jnp.asarray(cycle[:, None] == cycle[None, :], jnp.bfloat16)
    reorder = jnp.asarray((cycle * n_frames + frame)[:, None] == index[None, :], jnp.bfloat16)
    blocks = pl.pallas_call(
        functools.partial(gram_kernel, n_pix, per_device, levels),
        out_shape=jax.ShapeDtypeStruct((ROWS, n_frames, n_frames), jnp.float32),
        in_specs=in_smem(3) + in_vmem(4 + 2 * n_pix),
        out_specs=in_vmem(1)[0],
        scratch_shapes=[
            pltpu.VMEM((width, slots), jnp.bfloat16),
            pltpu.VMEM((slots // LANES, levels * ROWS, LANES), jnp.float32),
        ],
        compiler_params=pltpu.CompilerParams(vmem_limit_bytes=VMEM_LIMIT),
        name="gram",
    )(place, dark_index, other_index, counts_col, counts_row, repeat, reorder, *received)
    n_half = n_frames // 2
    mine = lax.dynamic_slice_in_dim(blocks, core * n_half, n_half, 1)
    theirs = lax.ppermute(
        lax.dynamic_slice_in_dim(blocks, (1 - core) * n_half, n_half, 1), "tm", swap
    )
    lower = core == 0
    return jnp.concatenate(
        [jnp.where(lower, mine, theirs), jnp.where(lower, theirs, mine)], axis=0
    )


def solution(mesh):
    n_pix, n_tm = mesh.shape["pix"], mesh.shape["tm"]

    def local(frames, dark, dark_index, cycle_counts):
        owned, slots = frames.shape[1] // n_pix, frames.shape[2]
        fits = n_tm == 2 and owned == 2 * ROWS and n_pix & (n_pix - 1) == 0 and n_pix <= 8
        fits = fits and dark.shape[0] % 2 == 0 and dark.shape[2] % LANES == 0 and slots == dark.shape[2] * n_pix
        return (packed_local if fits else plain_local)(frames, dark, dark_index, cycle_counts)

    in_specs = (
        P(("parts", "tm", "pix"), None, None),
        P("parts", None, "pix"),
        P(("parts", "tm")),
        P(),
    )
    out_specs = P("pix", ("parts", "tm"), None)
    return jax.shard_map(local, mesh=mesh, in_specs=in_specs, out_specs=out_specs, check_vma=False)
```

```python
import functools

import jax
import jax.numpy as jnp
from jax import lax
from jax.experimental import pallas as pl
from jax.experimental.pallas import tpu as pltpu
from jax.sharding import PartitionSpec as P

LANES = 128
ROWS = 16
VMEM_LIMIT = 16 * 1024 * 1024


def subtract_dark(raw_frames, dark_frames, dark_index, live_slot):
    values = raw_frames.astype(jnp.float32)
    for dark_level in range(dark_frames.shape[0]):
        picked = (dark_index == dark_level)[:, None, None]
        values = values - jnp.where(
            picked, dark_frames[dark_level].astype(jnp.float32)[None], jnp.float32(0.0)
        )
    return jnp.where(live_slot[None], values, jnp.float32(0.0)).astype(jnp.bfloat16)


def correlate(row_signal, col_signal):
    gram_tiles = jnp.einsum(
        "tqs,uqs->qtu", row_signal, col_signal, preferred_element_type=jnp.float32
    )
    totals = jnp.sum(col_signal, axis=2, dtype=jnp.float32).T
    return (gram_tiles, totals)


def plain_local(frames, dark, dark_index, cycle_counts):
    pix_count = lax.axis_size("pix")
    pix_index = lax.axis_index("pix")
    tm_index = lax.axis_index("tm")
    owned_cycles = frames.shape[1] // pix_count
    regrouped = lax.all_to_all(frames, "pix", split_axis=1, concat_axis=0, tiled=True)
    dark_cycles = lax.all_to_all(dark, "pix", split_axis=1, concat_axis=2, tiled=True)
    block_counts = lax.dynamic_slice_in_dim(cycle_counts, pix_index * owned_cycles, owned_cycles, 0)
    live_slot = jnp.arange(regrouped.shape[2], dtype=jnp.int32)[None, :] < block_counts[:, None]
    signal = subtract_dark(regrouped, dark_cycles, dark_index, live_slot)
    half_frames = signal.shape[0]
    all_frames = lax.all_gather(signal, "tm", axis=0, tiled=True)
    gram_tiles, totals = correlate(signal, all_frames)
    live_counts = lax.dynamic_slice_in_dim(
        cycle_counts, pix_index * owned_cycles, owned_cycles, 0
    ).astype(jnp.float32)
    row_totals = lax.dynamic_slice_in_dim(totals, tm_index * half_frames, half_frames, 1)
    return gram_tiles * live_counts[:, None, None] / (row_totals[:, :, None] * totals[:, None, :])


def pack_kernel(n_pix, messages, place, frames, dark, *refs):
    count = len(messages)
    outs, (raw, shade, raw_sem, shade_sem) = refs[:count], refs[count:]
    per_device, slots = frames.shape[0], frames.shape[-1]
    share = shade.shape[1]
    copies = []
    for n, k in enumerate(messages):
        dest, half = place[0] ^ (k % n_pix), place[1] ^ (k // n_pix)
        copies.append((
            pltpu.make_async_copy(frames.at[:, dest, half], raw.at[n], raw_sem.at[n]),
            pltpu.make_async_copy(
                dark.at[pl.ds(place[1] * share, share), dest, half], shade.at[n], shade_sem.at[n]
            ),
        ))
        for copy in copies[-1]:
            copy.start()
    for n in range(count):
        for copy in copies[n]:
            copy.wait()
        row = 0
        for block, depth in ((raw, per_device), (shade, share)):
            for f in range(depth):
                for j in range(block.shape[-1] // LANES):
                    outs[n][pl.ds(row, ROWS), :] = block[n, f, :, pl.ds(j * LANES, LANES)]
                    row += ROWS


def split3(x):
    high = x.astype(jnp.bfloat16)
    rest = x - high.astype(jnp.float32)
    middle = rest.astype(jnp.bfloat16)
    low = (rest - middle.astype(jnp.float32)).astype(jnp.bfloat16)
    return high, middle, low


def pick(x, chosen):
    return sum(jnp.dot(part, chosen, preferred_element_type=jnp.float32) for part in split3(x))


def gram_kernel(n_pix, per_device, levels, order, place, own_index, other_index, cycle_counts, *refs):
    n_bufs = 2 * n_pix
    bufs, (mine, theirs, signal, dark) = dict(zip(order, refs)), refs[n_bufs:]
    me, core = place[0], place[1]
    share = levels // 2
    frames_half = per_device * n_pix
    n_frames = 2 * frames_half
    slots = signal.shape[1]
    tiles = slots // LANES
    dark_tiles = tiles // n_pix
    dark_row = per_device * tiles * ROWS
    lane = lax.broadcasted_iota(jnp.int32, (ROWS, LANES), 1)
    cycle = lax.broadcasted_iota(jnp.int32, (ROWS, LANES), 0)
    counts = jnp.zeros((ROWS, LANES), jnp.int32)
    for q in range(ROWS):
        count = cycle_counts[(2 * me + core) * ROWS + q]
        counts = jnp.where(cycle == q, count, counts)
    live = [lane + j * LANES < counts for j in range(tiles)]
    for k in range(n_bufs):
        source, half = me ^ (k % n_pix), core ^ (k // n_pix)
        for j in range(dark_tiles):
            for n in range(share):
                level = pl.multiple_of((half * share + n) * ROWS, ROWS)
                row = dark_row + (n * dark_tiles + j) * ROWS
                dark[source * dark_tiles + j, pl.ds(level, ROWS), :] = bufs[k][
                    pl.ds(row, ROWS), :
                ].astype(jnp.float32)
    for k in range(n_bufs):
        source, half = me ^ (k % n_pix), core ^ (k // n_pix)
        index = own_index if k < n_pix else other_index
        for f in range(per_device):
            frame = source * per_device + f
            first = pl.multiple_of(((k // n_pix) * frames_half + frame) * ROWS, ROWS)
            dark_first = pl.multiple_of(index[frame] * ROWS, ROWS)
            for j in range(tiles):
                raw = bufs[k][pl.ds((f * tiles + j) * ROWS, ROWS), :].astype(jnp.float32)
                value = raw - dark[j, pl.ds(dark_first, ROWS), :]
                value = jnp.where(live[j], value, 0.0)
                signal[pl.ds(first, ROWS), pl.ds(j * LANES, LANES)] = value.astype(jnp.bfloat16)
    contract = (((1,), (1,)), ((), ()))
    width = n_frames * ROWS
    every = signal[...]
    totals = lax.dot_general(
        jnp.ones((ROWS, slots), jnp.bfloat16), every, contract, preferred_element_type=jnp.float32
    )
    products = lax.dot_general(every, every, contract, preferred_element_type=jnp.float32)
    products = jnp.concatenate([products, totals], axis=0)
    row = lax.broadcasted_iota(jnp.int32, products.shape, 0)
    col = lax.broadcasted_iota(jnp.int32, products.shape, 1)
    products = jnp.where(row % ROWS == col % ROWS, products, 0.0)
    frame = lax.broadcasted_iota(jnp.int32, (width, LANES), 0) // ROWS
    lane = lax.broadcasted_iota(jnp.int32, (width, LANES), 1)
    place_out = (frame + core * frames_half) % n_frames
    fold = jnp.where((lane == place_out) | (lane == frame + n_frames), 1.0, 0.0)
    folded = pick(products, fold.astype(jnp.bfloat16))
    totals = folded[width:]
    counts = counts.astype(jnp.float32)[:, :n_frames]
    for t in range(n_frames):
        scale = totals[:, n_frames + t : n_frames + t + 1] * totals[:, :n_frames]
        block = folded[t * ROWS : (t + 1) * ROWS, :n_frames] * counts / scale
        out = mine if t < frames_half else theirs
        out[:, t % frames_half, :] = block


def in_vmem(count):
    return [pl.BlockSpec(memory_space=pltpu.VMEM)] * count


def in_smem(count):
    return [pl.BlockSpec(memory_space=pltpu.SMEM)] * count


def packed_local(frames, dark, dark_index, cycle_counts):
    n_pix, core, me = lax.axis_size("pix"), lax.axis_index("tm"), lax.axis_index("pix")
    per_device, _, slots = frames.shape
    levels, _, dark_slots = dark.shape
    n_frames = 2 * per_device * n_pix
    swap = [(0, 1), (1, 0)]
    split_frames = pltpu.with_memory_space_constraint(
        frames.reshape(per_device, n_pix, 2, ROWS, slots), pltpu.HBM
    )
    split_dark = pltpu.with_memory_space_constraint(
        dark.reshape(levels, n_pix, 2, ROWS, dark_slots), pltpu.HBM
    )
    share = levels // 2
    place = jnp.stack([me, core]).astype(jnp.int32)
    rows = (per_device * slots + share * dark_slots) // LANES * ROWS
    half = n_pix // 2
    far = [t * n_pix + k for t in range(2) for k in range(half, n_pix)]
    near = [t * n_pix + k for t in range(2) for k in range(1, half)] + [n_pix]
    order = [k for pair in zip(far, near) for k in pair] + far[len(near) :]
    messages = order + [0]
    count = len(messages)
    packed = pl.pallas_call(
        functools.partial(pack_kernel, n_pix, messages),
        out_shape=[jax.ShapeDtypeStruct((rows, LANES), frames.dtype)] * count,
        in_specs=in_smem(1) + [pl.BlockSpec(memory_space=pltpu.HBM)] * 2,
        out_specs=in_vmem(count),
        scratch_shapes=[
            pltpu.VMEM((count, per_device, ROWS, slots), frames.dtype),
            pltpu.VMEM((count, share, ROWS, dark_slots), dark.dtype),
            pltpu.SemaphoreType.DMA((count,)),
            pltpu.SemaphoreType.DMA((count,)),
        ],
        compiler_params=pltpu.CompilerParams(vmem_limit_bytes=VMEM_LIMIT),
        name="pack",
    )(place, split_frames, split_dark)
    received = [
        lax.ppermute(buffer, ("tm", "pix"), [(i, i ^ k) for i in range(2 * n_pix)]) if k else buffer
        for k, buffer in zip(messages, packed)
    ]
    other_index = lax.ppermute(dark_index, "tm", swap)
    width = n_frames * ROWS
    blocks = jax.ShapeDtypeStruct((ROWS, n_frames // 2, n_frames), jnp.float32)
    mine, send = pl.pallas_call(
        functools.partial(gram_kernel, n_pix, per_device, levels, messages),
        out_shape=[blocks, blocks],
        in_specs=in_smem(4) + in_vmem(2 * n_pix),
        out_specs=in_vmem(2),
        scratch_shapes=[
            pltpu.VMEM((width, slots), jnp.bfloat16),
            pltpu.VMEM((slots // LANES, levels * ROWS, LANES), jnp.float32),
        ],
        compiler_params=pltpu.CompilerParams(vmem_limit_bytes=VMEM_LIMIT),
        name="gram",
    )(place, dark_index, other_index, cycle_counts, *received)
    theirs = lax.ppermute(send, "tm", swap)
    lower = core == 0
    return jnp.concatenate(
        [jnp.where(lower, mine, theirs), jnp.where(lower, theirs, mine)], axis=0
    )


def solution(mesh):
    n_pix, n_tm = mesh.shape["pix"], mesh.shape["tm"]

    def local(frames, dark, dark_index, cycle_counts):
        owned, slots = frames.shape[1] // n_pix, frames.shape[2]
        fits = n_tm == 2 and owned == 2 * ROWS and n_pix & (n_pix - 1) == 0 and n_pix <= 8
        fits = fits and dark.shape[0] % 2 == 0 and dark.shape[2] % LANES == 0 and slots == dark.shape[2] * n_pix
        return (packed_local if fits else plain_local)(frames, dark, dark_index, cycle_counts)

    in_specs = (
        P(("parts", "tm", "pix"), None, None),
        P("parts", None, "pix"),
        P(("parts", "tm")),
        P(),
    )
    out_specs = P("pix", ("parts", "tm"), None)
    return jax.shard_map(local, mesh=mesh, in_specs=in_specs, out_specs=out_specs, check_vma=False)
```

```python
import functools

import jax
import jax.numpy as jnp
from jax import lax
from jax.experimental import pallas as pl
from jax.experimental.pallas import tpu as pltpu
from jax.sharding import PartitionSpec as P

LANES = 128
ROWS = 16
FIRST = 2
ROOMS = (9, 10, 11, 12, 13)
VMEM_LIMIT = 16 * 1024 * 1024


def subtract_dark(raw_frames, dark_frames, dark_index, live_slot):
    values = raw_frames.astype(jnp.float32)
    for dark_level in range(dark_frames.shape[0]):
        picked = (dark_index == dark_level)[:, None, None]
        values = values - jnp.where(
            picked, dark_frames[dark_level].astype(jnp.float32)[None], jnp.float32(0.0)
        )
    return jnp.where(live_slot[None], values, jnp.float32(0.0)).astype(jnp.bfloat16)


def correlate(row_signal, col_signal):
    gram_tiles = jnp.einsum(
        "tqs,uqs->qtu", row_signal, col_signal, preferred_element_type=jnp.float32
    )
    totals = jnp.sum(col_signal, axis=2, dtype=jnp.float32).T
    return (gram_tiles, totals)


def plain_local(frames, dark, dark_index, cycle_counts):
    pix_count = lax.axis_size("pix")
    pix_index = lax.axis_index("pix")
    tm_index = lax.axis_index("tm")
    owned_cycles = frames.shape[1] // pix_count
    regrouped = lax.all_to_all(frames, "pix", split_axis=1, concat_axis=0, tiled=True)
    dark_cycles = lax.all_to_all(dark, "pix", split_axis=1, concat_axis=2, tiled=True)
    block_counts = lax.dynamic_slice_in_dim(cycle_counts, pix_index * owned_cycles, owned_cycles, 0)
    live_slot = jnp.arange(regrouped.shape[2], dtype=jnp.int32)[None, :] < block_counts[:, None]
    signal = subtract_dark(regrouped, dark_cycles, dark_index, live_slot)
    half_frames = signal.shape[0]
    all_frames = lax.all_gather(signal, "tm", axis=0, tiled=True)
    gram_tiles, totals = correlate(signal, all_frames)
    live_counts = lax.dynamic_slice_in_dim(
        cycle_counts, pix_index * owned_cycles, owned_cycles, 0
    ).astype(jnp.float32)
    row_totals = lax.dynamic_slice_in_dim(totals, tm_index * half_frames, half_frames, 1)
    return gram_tiles * live_counts[:, None, None] / (row_totals[:, :, None] * totals[:, None, :])


def plan_kernel(rooms, slots, counts, position, branch):
    receivers, units = position.shape
    every = counts[...].astype(jnp.float32)
    own = (
        lax.broadcasted_iota(jnp.int32, (receivers, every.shape[1]), 1) // ROWS
        == lax.broadcasted_iota(jnp.int32, (receivers, every.shape[1]), 0)
    )
    repeat = (
        lax.broadcasted_iota(jnp.int32, (every.shape[1], units), 0) % ROWS
        == lax.broadcasted_iota(jnp.int32, (every.shape[1], units), 1) % ROWS
    )
    count = pick(jnp.where(own, every, 0.0), jnp.where(repeat, 1.0, 0.0).astype(jnp.bfloat16))
    tile = lax.broadcasted_iota(jnp.int32, (receivers, units), 1) // ROWS
    live = count > (slots // 2 + tile * LANES).astype(jnp.float32)
    flags = jnp.where(live, 1.0, 0.0)
    before = (
        lax.broadcasted_iota(jnp.int32, (units, units), 0)
        < lax.broadcasted_iota(jnp.int32, (units, units), 1)
    )
    place = jnp.dot(
        flags.astype(jnp.bfloat16),
        jnp.where(before, 1.0, 0.0).astype(jnp.bfloat16),
        preferred_element_type=jnp.float32,
    )
    position[...] = jnp.where(live, place, -1.0)
    most = jnp.max(jnp.sum(flags, axis=1, keepdims=True)).astype(jnp.int32)
    branch[0] = sum(jnp.where(most > room, 1, 0) for room in rooms[:-1])


def chooser(position, receiver, room):
    units = position.shape[1]
    row = lax.broadcasted_iota(jnp.int32, (room, units), 0).astype(jnp.float32)
    return jnp.where(row == position[pl.ds(receiver, 1), :], 1.0, 0.0)


def pack_kernel(n_pix, room, messages, after, place, position, frames, dark, *refs):
    count = len(messages)
    refs = refs[after:]
    outs, (raw, shade, raw_sem, shade_sem) = refs[:count], refs[count:]
    per_device, slots = frames.shape[0], frames.shape[-1]
    share = shade.shape[1]
    lower = slots // 2 // LANES
    units = lower * ROWS
    copies = []
    for n, k in enumerate(messages):
        dest, half = place[0] ^ (k % n_pix), place[1] ^ (k // n_pix)
        copies.append((
            pltpu.make_async_copy(frames.at[:, dest, half], raw.at[n], raw_sem.at[n]),
            pltpu.make_async_copy(
                dark.at[pl.ds(place[1] * share, share), dest, half], shade.at[n], shade_sem.at[n]
            ),
        ))
        for copy in copies[-1]:
            copy.start()
    for n, k in enumerate(messages):
        for copy in copies[n]:
            copy.wait()
        row = 0
        for block, depth, tiles in (
            (raw, per_device, range(lower)),
            (shade, share, range(shade.shape[-1] // LANES)),
            (raw, per_device, range(lower, 2 * lower) if room == units else ()),
        ):
            for f in range(depth):
                for j in tiles:
                    outs[n][pl.ds(row, ROWS), :] = block[n, f, :, pl.ds(j * LANES, LANES)]
                    row += ROWS
        if room < units:
            dest, half = place[0] ^ (k % n_pix), place[1] ^ (k // n_pix)
            chosen = chooser(position, dest * 2 + half, room).astype(jnp.bfloat16)
            upper = jnp.concatenate(
                [
                    jnp.concatenate(
                        [raw[n, f, :, pl.ds(j * LANES, LANES)] for j in range(lower, 2 * lower)], axis=0
                    )
                    for f in range(per_device)
                ],
                axis=1,
            )
            live = jnp.dot(chosen, upper, preferred_element_type=jnp.float32)
            live = jnp.concatenate(
                [live[:, f * LANES : (f + 1) * LANES] for f in range(per_device)], axis=0
            )
            outs[n][pl.ds(row, per_device * room), :] = live.astype(jnp.bfloat16)


def split3(x):
    high = x.astype(jnp.bfloat16)
    rest = x - high.astype(jnp.float32)
    middle = rest.astype(jnp.bfloat16)
    low = (rest - middle.astype(jnp.float32)).astype(jnp.bfloat16)
    return high, middle, low


def pick(x, chosen):
    return sum(jnp.dot(part, chosen, preferred_element_type=jnp.float32) for part in split3(x))


def gram_kernel(
    n_pix, per_device, levels, room, order, place, own_index, other_index, cycle_counts, position, *refs
):
    n_bufs = 2 * n_pix
    bufs, (mine, theirs, signal, dark) = dict(zip(order, refs)), refs[n_bufs:]
    me, core = place[0], place[1]
    share = levels // 2
    frames_half = per_device * n_pix
    n_frames = 2 * frames_half
    slots = signal.shape[1]
    tiles = slots // LANES
    dark_tiles = tiles // n_pix
    lower = tiles // 2
    units = lower * ROWS
    dark_row = per_device * units
    upper_row = dark_row + share * dark_tiles * ROWS
    if room < units:
        chosen = chooser(position, me * 2 + core, units).T.astype(jnp.bfloat16)[:, :room]
    lane = lax.broadcasted_iota(jnp.int32, (ROWS, LANES), 1)
    cycle = lax.broadcasted_iota(jnp.int32, (ROWS, LANES), 0)
    counts = jnp.zeros((ROWS, LANES), jnp.int32)
    for q in range(ROWS):
        count = cycle_counts[(2 * me + core) * ROWS + q]
        counts = jnp.where(cycle == q, count, counts)
    live = [lane + j * LANES < counts for j in range(tiles)]
    for k in range(n_bufs):
        source, half = me ^ (k % n_pix), core ^ (k // n_pix)
        for j in range(dark_tiles):
            for n in range(share):
                level = pl.multiple_of((half * share + n) * ROWS, ROWS)
                row = dark_row + (n * dark_tiles + j) * ROWS
                dark[source * dark_tiles + j, pl.ds(level, ROWS), :] = bufs[k][
                    pl.ds(row, ROWS), :
                ].astype(jnp.float32)
    for k in range(n_bufs):
        source, half = me ^ (k % n_pix), core ^ (k // n_pix)
        index = own_index if k < n_pix else other_index
        if room < units:
            packed = [bufs[k][pl.ds(upper_row + f * room, room), :] for f in range(per_device)]
            upper = jnp.dot(
                chosen, jnp.concatenate(packed, axis=1), preferred_element_type=jnp.float32
            )
        for f in range(per_device):
            frame = source * per_device + f
            first = pl.multiple_of(((k // n_pix) * frames_half + frame) * ROWS, ROWS)
            dark_first = pl.multiple_of(index[frame] * ROWS, ROWS)
            for j in range(tiles):
                unit = (j % lower) * ROWS
                if j < lower:
                    raw = bufs[k][pl.ds(f * units + unit, ROWS), :].astype(jnp.float32)
                elif room < units:
                    raw = upper[unit : unit + ROWS, f * LANES : (f + 1) * LANES]
                else:
                    raw = bufs[k][pl.ds(upper_row + f * units + unit, ROWS), :].astype(jnp.float32)
                value = raw - dark[j, pl.ds(dark_first, ROWS), :]
                value = jnp.where(live[j], value, 0.0)
                signal[pl.ds(first, ROWS), pl.ds(j * LANES, LANES)] = value.astype(jnp.bfloat16)
    contract = (((1,), (1,)), ((), ()))
    width = n_frames * ROWS
    every = signal[...]
    totals = lax.dot_general(
        jnp.ones((ROWS, slots), jnp.bfloat16), every, contract, preferred_element_type=jnp.float32
    )
    products = lax.dot_general(every, every, contract, preferred_element_type=jnp.float32)
    products = jnp.concatenate([products, totals], axis=0)
    row = lax.broadcasted_iota(jnp.int32, products.shape, 0)
    col = lax.broadcasted_iota(jnp.int32, products.shape, 1)
    products = jnp.where(row % ROWS == col % ROWS, products, 0.0)
    frame = lax.broadcasted_iota(jnp.int32, (width, LANES), 0) // ROWS
    lane = lax.broadcasted_iota(jnp.int32, (width, LANES), 1)
    place_out = (frame + core * frames_half) % n_frames
    fold = jnp.where((lane == place_out) | (lane == frame + n_frames), 1.0, 0.0)
    folded = pick(products, fold.astype(jnp.bfloat16))
    totals = folded[width:]
    counts = counts.astype(jnp.float32)[:, :n_frames]
    for t in range(n_frames):
        scale = totals[:, n_frames + t : n_frames + t + 1] * totals[:, :n_frames]
        block = folded[t * ROWS : (t + 1) * ROWS, :n_frames] * counts / scale
        out = mine if t < frames_half else theirs
        out[:, t % frames_half, :] = block


def in_vmem(count):
    return [pl.BlockSpec(memory_space=pltpu.VMEM)] * count


def in_smem(count):
    return [pl.BlockSpec(memory_space=pltpu.SMEM)] * count


def packed_local(frames, dark, dark_index, cycle_counts):
    n_pix, core, me = lax.axis_size("pix"), lax.axis_index("tm"), lax.axis_index("pix")
    per_device, _, slots = frames.shape
    levels, _, dark_slots = dark.shape
    n_frames = 2 * per_device * n_pix
    share = levels // 2
    units = slots // 2 // LANES * ROWS
    rooms = [units * part // 16 for part in ROOMS] + [units]
    swap = [(0, 1), (1, 0)]
    half = n_pix // 2
    far = [t * n_pix + k for t in range(2) for k in [*range(half, n_pix, 2), *range(half + 1, n_pix, 2)]]
    near = [t * n_pix + k for t in range(2) for k in range(1, half)] + [n_pix]
    order = far[:1] + [k for pair in zip(far[1:], near) for k in pair]
    messages = order + [0]
    count = len(messages)

    def exchange(room, place, position, frames, dark, own_index, other_index, cycle_counts):
        rows = per_device * (units + room) + share * dark_slots // LANES * ROWS
        packed = []
        for group in (messages[:FIRST], messages[FIRST:]):
            size, after = len(group), packed[:1]
            packed += pl.pallas_call(
                functools.partial(pack_kernel, n_pix, room, group, len(after)),
                out_shape=[jax.ShapeDtypeStruct((rows, LANES), frames.dtype)] * size,
                in_specs=in_smem(1) + in_vmem(1)
                + [pl.BlockSpec(memory_space=pltpu.HBM)] * 2
                + [pl.BlockSpec(memory_space=pl.ANY)] * len(after),
                out_specs=in_vmem(size),
                scratch_shapes=[
                    pltpu.VMEM((size, per_device, ROWS, slots), frames.dtype),
                    pltpu.VMEM((size, share, ROWS, dark_slots), dark.dtype),
                    pltpu.SemaphoreType.DMA((size,)),
                    pltpu.SemaphoreType.DMA((size,)),
                ],
                compiler_params=pltpu.CompilerParams(vmem_limit_bytes=VMEM_LIMIT),
                name="pack",
            )(
                place,
                position,
                pltpu.with_memory_space_constraint(frames, pltpu.HBM),
                pltpu.with_memory_space_constraint(dark, pltpu.HBM),
                *after,
            )
        received = [
            lax.ppermute(buffer, ("tm", "pix"), [(i, i ^ k) for i in range(count)]) if k else buffer
            for k, buffer in zip(messages, packed)
        ]
        blocks = jax.ShapeDtypeStruct((ROWS, n_frames // 2, n_frames), jnp.float32)
        mine, send = pl.pallas_call(
            functools.partial(gram_kernel, n_pix, per_device, levels, room, messages),
            out_shape=[blocks, blocks],
            in_specs=in_smem(4) + in_vmem(1 + count),
            out_specs=in_vmem(2),
            scratch_shapes=[
                pltpu.VMEM((n_frames * ROWS, slots), jnp.bfloat16),
                pltpu.VMEM((slots // LANES, levels * ROWS, LANES), jnp.float32),
            ],
            compiler_params=pltpu.CompilerParams(vmem_limit_bytes=VMEM_LIMIT),
            name="gram",
        )(place, own_index, other_index, cycle_counts, position, *received)
        return mine, send

    place = jnp.stack([me, core]).astype(jnp.int32)
    position, branch = pl.pallas_call(
        functools.partial(plan_kernel, rooms, slots),
        out_shape=[
            jax.ShapeDtypeStruct((2 * n_pix, units), jnp.float32),
            jax.ShapeDtypeStruct((1,), jnp.int32),
        ],
        in_specs=in_vmem(1),
        out_specs=in_vmem(1) + in_smem(1),
        name="plan",
    )(cycle_counts.reshape(1, -1))
    other_index = lax.ppermute(dark_index, "tm", swap)
    mine, send = lax.switch(
        branch[0],
        [functools.partial(exchange, room) for room in rooms],
        place,
        position,
        frames.reshape(per_device, n_pix, 2, ROWS, slots),
        dark.reshape(levels, n_pix, 2, ROWS, dark_slots),
        dark_index,
        other_index,
        cycle_counts,
    )
    theirs = lax.ppermute(send, "tm", swap)
    lower = core == 0
    return jnp.concatenate(
        [jnp.where(lower, mine, theirs), jnp.where(lower, theirs, mine)], axis=0
    )


def solution(mesh):
    n_pix, n_tm = mesh.shape["pix"], mesh.shape["tm"]

    def local(frames, dark, dark_index, cycle_counts):
        owned, slots = frames.shape[1] // n_pix, frames.shape[2]
        fits = n_tm == 2 and owned == 2 * ROWS and slots % (2 * LANES) == 0 and n_pix & (n_pix - 1) == 0 and n_pix <= 8
        fits = fits and dark.shape[0] % 2 == 0 and dark.shape[2] % LANES == 0 and slots == dark.shape[2] * n_pix
        return (packed_local if fits else plain_local)(frames, dark, dark_index, cycle_counts)

    in_specs = (
        P(("parts", "tm", "pix"), None, None),
        P("parts", None, "pix"),
        P(("parts", "tm")),
        P(),
    )
    out_specs = P("pix", ("parts", "tm"), None)
    return jax.shard_map(local, mesh=mesh, in_specs=in_specs, out_specs=out_specs, check_vma=False)
```

```python
import functools

import jax
import jax.numpy as jnp
from jax import lax
from jax.experimental import pallas as pl
from jax.experimental.pallas import tpu as pltpu
from jax.sharding import PartitionSpec as P

LANES = 128
ROWS = 16
FIRST = 2
ROOMS = (9, 10, 11, 12, 13)
VMEM_LIMIT = 16 * 1024 * 1024


def subtract_dark(raw_frames, dark_frames, dark_index, live_slot):
    values = raw_frames.astype(jnp.float32)
    for dark_level in range(dark_frames.shape[0]):
        picked = (dark_index == dark_level)[:, None, None]
        values = values - jnp.where(
            picked, dark_frames[dark_level].astype(jnp.float32)[None], jnp.float32(0.0)
        )
    return jnp.where(live_slot[None], values, jnp.float32(0.0)).astype(jnp.bfloat16)


def correlate(row_signal, col_signal):
    gram_tiles = jnp.einsum(
        "tqs,uqs->qtu", row_signal, col_signal, preferred_element_type=jnp.float32
    )
    totals = jnp.sum(col_signal, axis=2, dtype=jnp.float32).T
    return (gram_tiles, totals)


def plain_local(frames, dark, dark_index, cycle_counts):
    pix_count = lax.axis_size("pix")
    pix_index = lax.axis_index("pix")
    tm_index = lax.axis_index("tm")
    owned_cycles = frames.shape[1] // pix_count
    regrouped = lax.all_to_all(frames, "pix", split_axis=1, concat_axis=0, tiled=True)
    dark_cycles = lax.all_to_all(dark, "pix", split_axis=1, concat_axis=2, tiled=True)
    block_counts = lax.dynamic_slice_in_dim(cycle_counts, pix_index * owned_cycles, owned_cycles, 0)
    live_slot = jnp.arange(regrouped.shape[2], dtype=jnp.int32)[None, :] < block_counts[:, None]
    signal = subtract_dark(regrouped, dark_cycles, dark_index, live_slot)
    half_frames = signal.shape[0]
    all_frames = lax.all_gather(signal, "tm", axis=0, tiled=True)
    gram_tiles, totals = correlate(signal, all_frames)
    live_counts = lax.dynamic_slice_in_dim(
        cycle_counts, pix_index * owned_cycles, owned_cycles, 0
    ).astype(jnp.float32)
    row_totals = lax.dynamic_slice_in_dim(totals, tm_index * half_frames, half_frames, 1)
    return gram_tiles * live_counts[:, None, None] / (row_totals[:, :, None] * totals[:, None, :])


def plan_kernel(rooms, slots, counts, position, branch):
    receivers, units = position.shape
    every = (jnp.maximum(counts[...] - slots // 2, 0) + LANES - 1) // LANES
    own = (
        lax.broadcasted_iota(jnp.int32, (receivers, every.shape[1]), 1) // ROWS
        == lax.broadcasted_iota(jnp.int32, (receivers, every.shape[1]), 0)
    )
    repeat = (
        lax.broadcasted_iota(jnp.int32, (every.shape[1], units), 0) % ROWS
        == lax.broadcasted_iota(jnp.int32, (every.shape[1], units), 1) % ROWS
    )
    number = jnp.dot(
        jnp.where(own, every, 0).astype(jnp.float32).astype(jnp.bfloat16),
        jnp.where(repeat, 1.0, 0.0).astype(jnp.bfloat16),
        preferred_element_type=jnp.float32,
    )
    tile = lax.broadcasted_iota(jnp.int32, (receivers, units), 1) // ROWS
    live = tile.astype(jnp.float32) < number
    flags = jnp.where(live, 1.0, 0.0)
    before = (
        lax.broadcasted_iota(jnp.int32, (units, units), 0)
        < lax.broadcasted_iota(jnp.int32, (units, units), 1)
    )
    place = jnp.dot(
        flags.astype(jnp.bfloat16),
        jnp.where(before, 1.0, 0.0).astype(jnp.bfloat16),
        preferred_element_type=jnp.float32,
    )
    position[...] = jnp.where(live, place, -1.0)
    most = jnp.max(jnp.sum(flags, axis=1, keepdims=True)).astype(jnp.int32)
    branch[0] = sum(jnp.where(most > room, 1, 0) for room in rooms[:-1])


def chooser(position, receiver, room):
    units = position.shape[1]
    row = lax.broadcasted_iota(jnp.int32, (room, units), 0).astype(jnp.float32)
    return jnp.where(row == position[pl.ds(receiver, 1), :], 1.0, 0.0)


def pack_kernel(n_pix, room, messages, after, place, position, frames, dark, *refs):
    count = len(messages)
    refs = refs[after:]
    outs, (raw, shade, raw_sem, shade_sem) = refs[:count], refs[count:]
    per_device, slots = frames.shape[0], frames.shape[-1]
    share = shade.shape[1]
    lower = slots // 2 // LANES
    units = lower * ROWS
    copies = []
    for n, k in enumerate(messages):
        dest, half = place[0] ^ (k % n_pix), place[1] ^ (k // n_pix)
        copies.append((
            pltpu.make_async_copy(frames.at[:, dest, half], raw.at[n], raw_sem.at[n]),
            pltpu.make_async_copy(
                dark.at[pl.ds(place[1] * share, share), dest, half], shade.at[n], shade_sem.at[n]
            ),
        ))
        for copy in copies[-1]:
            copy.start()
    for n, k in enumerate(messages):
        for copy in copies[n]:
            copy.wait()
        row = 0
        for block, depth, tiles in (
            (raw, per_device, range(lower)),
            (shade, share, range(shade.shape[-1] // LANES)),
            (raw, per_device, range(lower, 2 * lower) if room == units else ()),
        ):
            for f in range(depth):
                for j in tiles:
                    outs[n][pl.ds(row, ROWS), :] = block[n, f, :, pl.ds(j * LANES, LANES)]
                    row += ROWS
        if room < units:
            dest, half = place[0] ^ (k % n_pix), place[1] ^ (k // n_pix)
            chosen = chooser(position, dest * 2 + half, room).astype(jnp.bfloat16)
            upper = jnp.concatenate(
                [
                    jnp.concatenate(
                        [raw[n, f, :, pl.ds(j * LANES, LANES)] for j in range(lower, 2 * lower)], axis=0
                    )
                    for f in range(per_device)
                ],
                axis=1,
            )
            live = jnp.dot(chosen, upper, preferred_element_type=jnp.float32)
            live = jnp.concatenate(
                [live[:, f * LANES : (f + 1) * LANES] for f in range(per_device)], axis=0
            )
            outs[n][pl.ds(row, per_device * room), :] = live.astype(jnp.bfloat16)


def split3(x):
    high = x.astype(jnp.bfloat16)
    rest = x - high.astype(jnp.float32)
    middle = rest.astype(jnp.bfloat16)
    low = (rest - middle.astype(jnp.float32)).astype(jnp.bfloat16)
    return high, middle, low


def pick(x, chosen):
    return sum(jnp.dot(part, chosen, preferred_element_type=jnp.float32) for part in split3(x))


def gram_kernel(
    n_pix, per_device, levels, room, order, place, own_index, other_index, cycle_counts, position, *refs
):
    n_bufs = 2 * n_pix
    bufs, (mine, theirs, signal, dark) = dict(zip(order, refs)), refs[n_bufs:]
    me, core = place[0], place[1]
    share = levels // 2
    frames_half = per_device * n_pix
    n_frames = 2 * frames_half
    slots = signal.shape[1]
    tiles = slots // LANES
    dark_tiles = tiles // n_pix
    lower = tiles // 2
    units = lower * ROWS
    dark_row = per_device * units
    upper_row = dark_row + share * dark_tiles * ROWS
    if room < units:
        chosen = chooser(position, me * 2 + core, units).T.astype(jnp.bfloat16)[:, :room]
    lane = lax.broadcasted_iota(jnp.int32, (ROWS, LANES), 1)
    cycle = lax.broadcasted_iota(jnp.int32, (ROWS, LANES), 0)
    counts = jnp.zeros((ROWS, LANES), jnp.int32)
    for q in range(ROWS):
        count = cycle_counts[(2 * me + core) * ROWS + q]
        counts = jnp.where(cycle == q, count, counts)
    live = [lane + j * LANES < counts for j in range(tiles)]
    for k in range(n_bufs):
        source, half = me ^ (k % n_pix), core ^ (k // n_pix)
        for j in range(dark_tiles):
            for n in range(share):
                level = pl.multiple_of((half * share + n) * ROWS, ROWS)
                row = dark_row + (n * dark_tiles + j) * ROWS
                dark[source * dark_tiles + j, pl.ds(level, ROWS), :] = bufs[k][
                    pl.ds(row, ROWS), :
                ].astype(jnp.float32)
    for k in range(n_bufs):
        source, half = me ^ (k % n_pix), core ^ (k // n_pix)
        index = own_index if k < n_pix else other_index
        if room < units:
            packed = [bufs[k][pl.ds(upper_row + f * room, room), :] for f in range(per_device)]
            upper = jnp.dot(
                chosen, jnp.concatenate(packed, axis=1), preferred_element_type=jnp.float32
            )
        for f in range(per_device):
            frame = source * per_device + f
            first = pl.multiple_of(((k // n_pix) * frames_half + frame) * ROWS, ROWS)
            dark_first = pl.multiple_of(index[frame] * ROWS, ROWS)
            for j in range(tiles):
                unit = (j % lower) * ROWS
                if j < lower:
                    raw = bufs[k][pl.ds(f * units + unit, ROWS), :].astype(jnp.float32)
                elif room < units:
                    raw = upper[unit : unit + ROWS, f * LANES : (f + 1) * LANES]
                else:
                    raw = bufs[k][pl.ds(upper_row + f * units + unit, ROWS), :].astype(jnp.float32)
                value = raw - dark[j, pl.ds(dark_first, ROWS), :]
                value = jnp.where(live[j], value, 0.0)
                signal[pl.ds(first, ROWS), pl.ds(j * LANES, LANES)] = value.astype(jnp.bfloat16)
    contract = (((1,), (1,)), ((), ()))
    width = n_frames * ROWS
    every = signal[...]
    totals = lax.dot_general(
        jnp.ones((ROWS, slots), jnp.bfloat16), every, contract, preferred_element_type=jnp.float32
    )
    products = lax.dot_general(every, every, contract, preferred_element_type=jnp.float32)
    products = jnp.concatenate([products, totals], axis=0)
    row = lax.broadcasted_iota(jnp.int32, products.shape, 0)
    col = lax.broadcasted_iota(jnp.int32, products.shape, 1)
    products = jnp.where(row % ROWS == col % ROWS, products, 0.0)
    frame = lax.broadcasted_iota(jnp.int32, (width, LANES), 0) // ROWS
    lane = lax.broadcasted_iota(jnp.int32, (width, LANES), 1)
    place_out = (frame + core * frames_half) % n_frames
    fold = jnp.where((lane == place_out) | (lane == frame + n_frames), 1.0, 0.0)
    folded = pick(products, fold.astype(jnp.bfloat16))
    totals = folded[width:]
    counts = counts.astype(jnp.float32)[:, :n_frames]
    for t in range(n_frames):
        scale = totals[:, n_frames + t : n_frames + t + 1] * totals[:, :n_frames]
        block = folded[t * ROWS : (t + 1) * ROWS, :n_frames] * counts / scale
        out = mine if t < frames_half else theirs
        out[:, t % frames_half, :] = block


def in_vmem(count):
    return [pl.BlockSpec(memory_space=pltpu.VMEM)] * count


def in_smem(count):
    return [pl.BlockSpec(memory_space=pltpu.SMEM)] * count


def packed_local(frames, dark, dark_index, cycle_counts):
    n_pix, core, me = lax.axis_size("pix"), lax.axis_index("tm"), lax.axis_index("pix")
    per_device, _, slots = frames.shape
    levels, _, dark_slots = dark.shape
    n_frames = 2 * per_device * n_pix
    share = levels // 2
    units = slots // 2 // LANES * ROWS
    rooms = [units * part // 16 for part in ROOMS] + [units]
    swap = [(0, 1), (1, 0)]
    half = n_pix // 2
    far = [t * n_pix + k for t in range(2) for k in [*range(half, n_pix, 2), *range(half + 1, n_pix, 2)]]
    near = [t * n_pix + k for t in range(2) for k in range(1, half)] + [n_pix]
    order = far[:1] + [k for pair in zip(far[1:], near) for k in pair]
    messages = order + [0]
    count = len(messages)

    def exchange(room, place, position, frames, dark, own_index, cycle_counts):
        rows = per_device * (units + room) + share * dark_slots // LANES * ROWS
        packed = []
        for group in (messages[:FIRST], messages[FIRST:]):
            size, after = len(group), packed[:1]
            packed += pl.pallas_call(
                functools.partial(pack_kernel, n_pix, room, group, len(after)),
                out_shape=[jax.ShapeDtypeStruct((rows, LANES), frames.dtype)] * size,
                in_specs=in_smem(1) + in_vmem(1)
                + [pl.BlockSpec(memory_space=pltpu.HBM)] * 2
                + [pl.BlockSpec(memory_space=pl.ANY)] * len(after),
                out_specs=in_vmem(size),
                scratch_shapes=[
                    pltpu.VMEM((size, per_device, ROWS, slots), frames.dtype),
                    pltpu.VMEM((size, share, ROWS, dark_slots), dark.dtype),
                    pltpu.SemaphoreType.DMA((size,)),
                    pltpu.SemaphoreType.DMA((size,)),
                ],
                compiler_params=pltpu.CompilerParams(vmem_limit_bytes=VMEM_LIMIT),
                name="pack",
            )(
                place,
                position,
                pltpu.with_memory_space_constraint(frames, pltpu.HBM),
                pltpu.with_memory_space_constraint(dark, pltpu.HBM),
                *after,
            )
        other_index = lax.ppermute(own_index, "tm", swap)
        received = [
            lax.ppermute(buffer, ("tm", "pix"), [(i, i ^ k) for i in range(count)]) if k else buffer
            for k, buffer in zip(messages, packed)
        ]
        blocks = jax.ShapeDtypeStruct((ROWS, n_frames // 2, n_frames), jnp.float32)
        mine, send = pl.pallas_call(
            functools.partial(gram_kernel, n_pix, per_device, levels, room, messages),
            out_shape=[blocks, blocks],
            in_specs=in_smem(4) + in_vmem(1 + count),
            out_specs=in_vmem(2),
            scratch_shapes=[
                pltpu.VMEM((n_frames * ROWS, slots), jnp.bfloat16),
                pltpu.VMEM((slots // LANES, levels * ROWS, LANES), jnp.float32),
            ],
            compiler_params=pltpu.CompilerParams(vmem_limit_bytes=VMEM_LIMIT),
            name="gram",
        )(place, own_index, other_index, cycle_counts, position, *received)
        return mine, send

    place = jnp.stack([me, core]).astype(jnp.int32)
    position, branch = pl.pallas_call(
        functools.partial(plan_kernel, rooms, slots),
        out_shape=[
            jax.ShapeDtypeStruct((2 * n_pix, units), jnp.float32),
            jax.ShapeDtypeStruct((1,), jnp.int32),
        ],
        in_specs=in_vmem(1),
        out_specs=in_vmem(1) + in_smem(1),
        name="plan",
    )(cycle_counts.reshape(1, -1))
    mine, send = lax.switch(
        branch[0],
        [functools.partial(exchange, room) for room in rooms],
        place,
        position,
        frames.reshape(per_device, n_pix, 2, ROWS, slots),
        dark.reshape(levels, n_pix, 2, ROWS, dark_slots),
        dark_index,
        cycle_counts,
    )
    theirs = lax.ppermute(send, "tm", swap)
    lower = core == 0
    return jnp.concatenate(
        [jnp.where(lower, mine, theirs), jnp.where(lower, theirs, mine)], axis=0
    )


def solution(mesh):
    n_pix, n_tm = mesh.shape["pix"], mesh.shape["tm"]

    def local(frames, dark, dark_index, cycle_counts):
        owned, slots = frames.shape[1] // n_pix, frames.shape[2]
        fits = n_tm == 2 and owned == 2 * ROWS and slots % (2 * LANES) == 0 and n_pix & (n_pix - 1) == 0 and n_pix <= 8
        fits = fits and dark.shape[0] % 2 == 0 and dark.shape[2] % LANES == 0 and slots == dark.shape[2] * n_pix
        return (packed_local if fits else plain_local)(frames, dark, dark_index, cycle_counts)

    in_specs = (
        P(("parts", "tm", "pix"), None, None),
        P("parts", None, "pix"),
        P(("parts", "tm")),
        P(),
    )
    out_specs = P("pix", ("parts", "tm"), None)
    return jax.shard_map(local, mesh=mesh, in_specs=in_specs, out_specs=out_specs, check_vma=False)
```

```python
import functools

import jax
import jax.numpy as jnp
from jax import lax
from jax.experimental import pallas as pl
from jax.experimental.pallas import tpu as pltpu
from jax.sharding import PartitionSpec as P

LANES = 128
ROWS = 16
FIRST = 2
ROOMS = (9, 10, 11, 12, 13)
VMEM_LIMIT = 16 * 1024 * 1024


def subtract_dark(raw_frames, dark_frames, dark_index, live_slot):
    values = raw_frames.astype(jnp.float32)
    for dark_level in range(dark_frames.shape[0]):
        picked = (dark_index == dark_level)[:, None, None]
        values = values - jnp.where(
            picked, dark_frames[dark_level].astype(jnp.float32)[None], jnp.float32(0.0)
        )
    return jnp.where(live_slot[None], values, jnp.float32(0.0)).astype(jnp.bfloat16)


def correlate(row_signal, col_signal):
    gram_tiles = jnp.einsum(
        "tqs,uqs->qtu", row_signal, col_signal, preferred_element_type=jnp.float32
    )
    totals = jnp.sum(col_signal, axis=2, dtype=jnp.float32).T
    return (gram_tiles, totals)


def plain_local(frames, dark, dark_index, cycle_counts):
    pix_count = lax.axis_size("pix")
    pix_index = lax.axis_index("pix")
    tm_index = lax.axis_index("tm")
    owned_cycles = frames.shape[1] // pix_count
    regrouped = lax.all_to_all(frames, "pix", split_axis=1, concat_axis=0, tiled=True)
    dark_cycles = lax.all_to_all(dark, "pix", split_axis=1, concat_axis=2, tiled=True)
    block_counts = lax.dynamic_slice_in_dim(cycle_counts, pix_index * owned_cycles, owned_cycles, 0)
    live_slot = jnp.arange(regrouped.shape[2], dtype=jnp.int32)[None, :] < block_counts[:, None]
    signal = subtract_dark(regrouped, dark_cycles, dark_index, live_slot)
    half_frames = signal.shape[0]
    all_frames = lax.all_gather(signal, "tm", axis=0, tiled=True)
    gram_tiles, totals = correlate(signal, all_frames)
    live_counts = lax.dynamic_slice_in_dim(
        cycle_counts, pix_index * owned_cycles, owned_cycles, 0
    ).astype(jnp.float32)
    row_totals = lax.dynamic_slice_in_dim(totals, tm_index * half_frames, half_frames, 1)
    return gram_tiles * live_counts[:, None, None] / (row_totals[:, :, None] * totals[:, None, :])


def plan_kernel(rooms, slots, counts, position, branch):
    receivers, units = position.shape
    every = (jnp.maximum(counts[...] - slots // 2, 0) + LANES - 1) // LANES
    own = (
        lax.broadcasted_iota(jnp.int32, (receivers, every.shape[1]), 1) // ROWS
        == lax.broadcasted_iota(jnp.int32, (receivers, every.shape[1]), 0)
    )
    repeat = (
        lax.broadcasted_iota(jnp.int32, (every.shape[1], units), 0) % ROWS
        == lax.broadcasted_iota(jnp.int32, (every.shape[1], units), 1) % ROWS
    )
    number = jnp.dot(
        jnp.where(own, every, 0).astype(jnp.float32).astype(jnp.bfloat16),
        jnp.where(repeat, 1.0, 0.0).astype(jnp.bfloat16),
        preferred_element_type=jnp.float32,
    )
    tile = lax.broadcasted_iota(jnp.int32, (receivers, units), 1) // ROWS
    live = tile.astype(jnp.float32) < number
    flags = jnp.where(live, 1.0, 0.0)
    before = (
        lax.broadcasted_iota(jnp.int32, (units, units), 0)
        < lax.broadcasted_iota(jnp.int32, (units, units), 1)
    )
    place = jnp.dot(
        flags.astype(jnp.bfloat16),
        jnp.where(before, 1.0, 0.0).astype(jnp.bfloat16),
        preferred_element_type=jnp.float32,
    )
    position[...] = jnp.where(live, place, -1.0)
    most = jnp.max(jnp.sum(flags, axis=1, keepdims=True)).astype(jnp.int32)
    branch[0] = sum(jnp.where(most > room, 1, 0) for room in rooms[:-1])


def chooser(position, receiver, room):
    units = position.shape[1]
    row = lax.broadcasted_iota(jnp.int32, (room, units), 0).astype(jnp.float32)
    return jnp.where(row == position[pl.ds(receiver, 1), :], 1.0, 0.0)


def pack_kernel(n_pix, room, messages, after, place, position, frames, dark, *refs):
    count = len(messages)
    refs = refs[after:]
    outs, (raw, shade, raw_sem, shade_sem) = refs[:count], refs[count:]
    per_device, slots = frames.shape[0], frames.shape[-1]
    share = shade.shape[1]
    lower = slots // 2 // LANES
    units = lower * ROWS
    copies = []
    for n, k in enumerate(messages):
        dest, half = place[0] ^ (k % n_pix), place[1] ^ (k // n_pix)
        copies.append((
            pltpu.make_async_copy(frames.at[:, dest, half], raw.at[n], raw_sem.at[n]),
            pltpu.make_async_copy(
                dark.at[pl.ds(place[1] * share, share), dest, half], shade.at[n], shade_sem.at[n]
            ),
        ))
        for copy in copies[-1]:
            copy.start()
    for n, k in enumerate(messages):
        for copy in copies[n]:
            copy.wait()
        row = 0
        for block, depth, tiles in (
            (raw, per_device, range(lower)),
            (shade, share, range(shade.shape[-1] // LANES)),
            (raw, per_device, range(lower, 2 * lower) if room == units else ()),
        ):
            for f in range(depth):
                for j in tiles:
                    outs[n][pl.ds(row, ROWS), :] = block[n, f, :, pl.ds(j * LANES, LANES)]
                    row += ROWS
        if room < units:
            dest, half = place[0] ^ (k % n_pix), place[1] ^ (k // n_pix)
            chosen = chooser(position, dest * 2 + half, room).astype(jnp.bfloat16)
            upper = jnp.concatenate(
                [
                    jnp.concatenate(
                        [raw[n, f, :, pl.ds(j * LANES, LANES)] for j in range(lower, 2 * lower)], axis=0
                    )
                    for f in range(per_device)
                ],
                axis=1,
            )
            live = jnp.dot(chosen, upper, preferred_element_type=jnp.float32)
            live = jnp.concatenate(
                [live[:, f * LANES : (f + 1) * LANES] for f in range(per_device)], axis=0
            )
            outs[n][pl.ds(row, per_device * room), :] = live.astype(jnp.bfloat16)


def split3(x):
    high = x.astype(jnp.bfloat16)
    rest = x - high.astype(jnp.float32)
    middle = rest.astype(jnp.bfloat16)
    low = (rest - middle.astype(jnp.float32)).astype(jnp.bfloat16)
    return high, middle, low


def pick(x, chosen):
    return sum(jnp.dot(part, chosen, preferred_element_type=jnp.float32) for part in split3(x))


def gram_kernel(
    n_pix, per_device, levels, room, order, place, own_index, other_index, cycle_counts, position, *refs
):
    n_bufs = 2 * n_pix
    bufs, (mine, theirs, signal, dark) = dict(zip(order, refs)), refs[n_bufs:]
    me, core = place[0], place[1]
    share = levels // 2
    frames_half = per_device * n_pix
    n_frames = 2 * frames_half
    slots = signal.shape[1]
    tiles = slots // LANES
    dark_tiles = tiles // n_pix
    lower = tiles // 2
    units = lower * ROWS
    dark_row = per_device * units
    upper_row = dark_row + share * dark_tiles * ROWS
    if room < units:
        chosen = chooser(position, me * 2 + core, units).T.astype(jnp.bfloat16)[:, :room]
    lane = lax.broadcasted_iota(jnp.int32, (ROWS, LANES), 1)
    cycle = lax.broadcasted_iota(jnp.int32, (ROWS, LANES), 0)
    counts = jnp.zeros((ROWS, LANES), jnp.int32)
    for q in range(ROWS):
        count = cycle_counts[(2 * me + core) * ROWS + q]
        counts = jnp.where(cycle == q, count, counts)
    live = [lane + j * LANES < counts for j in range(tiles)]
    for k in range(n_bufs):
        source, half = me ^ (k % n_pix), core ^ (k // n_pix)
        for j in range(dark_tiles):
            for n in range(share):
                level = pl.multiple_of((half * share + n) * ROWS, ROWS)
                row = dark_row + (n * dark_tiles + j) * ROWS
                dark[source * dark_tiles + j, pl.ds(level, ROWS), :] = bufs[k][
                    pl.ds(row, ROWS), :
                ].astype(jnp.float32)
    for k in range(n_bufs):
        source, half = me ^ (k % n_pix), core ^ (k // n_pix)
        index = own_index if k < n_pix else other_index
        if room < units:
            packed = bufs[k][pl.ds(upper_row, per_device * room), :].astype(jnp.float32)
            packed = [packed[f * room : (f + 1) * room] for f in range(per_device)]
            upper = jnp.dot(
                chosen,
                jnp.concatenate(packed, axis=1).astype(jnp.bfloat16),
                preferred_element_type=jnp.float32,
            )
        for f in range(per_device):
            frame = source * per_device + f
            first = pl.multiple_of(((k // n_pix) * frames_half + frame) * ROWS, ROWS)
            dark_first = pl.multiple_of(index[frame] * ROWS, ROWS)
            for j in range(tiles):
                unit = (j % lower) * ROWS
                if j < lower:
                    raw = bufs[k][pl.ds(f * units + unit, ROWS), :].astype(jnp.float32)
                elif room < units:
                    raw = upper[unit : unit + ROWS, f * LANES : (f + 1) * LANES]
                else:
                    raw = bufs[k][pl.ds(upper_row + f * units + unit, ROWS), :].astype(jnp.float32)
                value = raw - dark[j, pl.ds(dark_first, ROWS), :]
                value = jnp.where(live[j], value, 0.0)
                signal[pl.ds(first, ROWS), pl.ds(j * LANES, LANES)] = value.astype(jnp.bfloat16)
    contract = (((1,), (1,)), ((), ()))
    width = n_frames * ROWS
    every = signal[...]
    totals = lax.dot_general(
        jnp.ones((ROWS, slots), jnp.bfloat16), every, contract, preferred_element_type=jnp.float32
    )
    products = lax.dot_general(every, every, contract, preferred_element_type=jnp.float32)
    products = jnp.concatenate([products, totals], axis=0)
    same = (
        lax.broadcasted_iota(jnp.int32, (ROWS, width), 0)
        == lax.broadcasted_iota(jnp.int32, (ROWS, width), 1) % ROWS
    )
    products = jnp.where(same[None], products.reshape(-1, ROWS, width), 0.0).reshape(-1, width)
    frame = lax.broadcasted_iota(jnp.int32, (width, LANES), 0) // ROWS
    lane = lax.broadcasted_iota(jnp.int32, (width, LANES), 1)
    place_out = (frame + core * frames_half) % n_frames
    fold = jnp.where((lane == place_out) | (lane == frame + n_frames), 1.0, 0.0)
    folded = pick(products, fold.astype(jnp.bfloat16))
    totals = folded[width:]
    counts = counts.astype(jnp.float32)[:, :n_frames]
    for t in range(n_frames):
        scale = totals[:, n_frames + t : n_frames + t + 1] * totals[:, :n_frames]
        block = folded[t * ROWS : (t + 1) * ROWS, :n_frames] * counts / scale
        out = mine if t < frames_half else theirs
        out[:, t % frames_half, :] = block


def in_vmem(count):
    return [pl.BlockSpec(memory_space=pltpu.VMEM)] * count


def in_smem(count):
    return [pl.BlockSpec(memory_space=pltpu.SMEM)] * count


def packed_local(frames, dark, dark_index, cycle_counts):
    n_pix, core, me = lax.axis_size("pix"), lax.axis_index("tm"), lax.axis_index("pix")
    per_device, _, slots = frames.shape
    levels, _, dark_slots = dark.shape
    n_frames = 2 * per_device * n_pix
    share = levels // 2
    units = slots // 2 // LANES * ROWS
    rooms = [units * part // 16 for part in ROOMS] + [units]
    swap = [(0, 1), (1, 0)]
    half = n_pix // 2
    far = [t * n_pix + k for t in range(2) for k in [*range(half, n_pix, 2), *range(half + 1, n_pix, 2)]]
    near = [t * n_pix + k for t in range(2) for k in range(1, half)] + [n_pix]
    order = far[:1] + [k for pair in zip(far[1:], near) for k in pair]
    messages = order + [0]
    count = len(messages)

    def exchange(room, place, position, frames, dark, own_index, cycle_counts):
        rows = per_device * (units + room) + share * dark_slots // LANES * ROWS
        packed = []
        for group in (messages[:FIRST], messages[FIRST:]):
            size, after = len(group), packed[:1]
            packed += pl.pallas_call(
                functools.partial(pack_kernel, n_pix, room, group, len(after)),
                out_shape=[jax.ShapeDtypeStruct((rows, LANES), frames.dtype)] * size,
                in_specs=in_smem(1) + in_vmem(1)
                + [pl.BlockSpec(memory_space=pltpu.HBM)] * 2
                + [pl.BlockSpec(memory_space=pl.ANY)] * len(after),
                out_specs=in_vmem(size),
                scratch_shapes=[
                    pltpu.VMEM((size, per_device, ROWS, slots), frames.dtype),
                    pltpu.VMEM((size, share, ROWS, dark_slots), dark.dtype),
                    pltpu.SemaphoreType.DMA((size,)),
                    pltpu.SemaphoreType.DMA((size,)),
                ],
                compiler_params=pltpu.CompilerParams(vmem_limit_bytes=VMEM_LIMIT),
                name="pack",
            )(
                place,
                position,
                pltpu.with_memory_space_constraint(frames, pltpu.HBM),
                pltpu.with_memory_space_constraint(dark, pltpu.HBM),
                *after,
            )
        other_index = lax.ppermute(own_index, "tm", swap)
        received = [
            lax.ppermute(buffer, ("tm", "pix"), [(i, i ^ k) for i in range(count)]) if k else buffer
            for k, buffer in zip(messages, packed)
        ]
        blocks = jax.ShapeDtypeStruct((ROWS, n_frames // 2, n_frames), jnp.float32)
        mine, send = pl.pallas_call(
            functools.partial(gram_kernel, n_pix, per_device, levels, room, messages),
            out_shape=[blocks, blocks],
            in_specs=in_smem(4) + in_vmem(1 + count),
            out_specs=in_vmem(2),
            scratch_shapes=[
                pltpu.VMEM((n_frames * ROWS, slots), jnp.bfloat16),
                pltpu.VMEM((slots // LANES, levels * ROWS, LANES), jnp.float32),
            ],
            compiler_params=pltpu.CompilerParams(vmem_limit_bytes=VMEM_LIMIT),
            name="gram",
        )(place, own_index, other_index, cycle_counts, position, *received)
        return mine, send

    place = jnp.stack([me, core]).astype(jnp.int32)
    position, branch = pl.pallas_call(
        functools.partial(plan_kernel, rooms, slots),
        out_shape=[
            jax.ShapeDtypeStruct((2 * n_pix, units), jnp.float32),
            jax.ShapeDtypeStruct((1,), jnp.int32),
        ],
        in_specs=in_vmem(1),
        out_specs=in_vmem(1) + in_smem(1),
        name="plan",
    )(cycle_counts.reshape(1, -1))
    mine, send = lax.switch(
        branch[0],
        [functools.partial(exchange, room) for room in rooms],
        place,
        position,
        frames.reshape(per_device, n_pix, 2, ROWS, slots),
        dark.reshape(levels, n_pix, 2, ROWS, dark_slots),
        dark_index,
        cycle_counts,
    )
    theirs = lax.ppermute(send, "tm", swap)
    lower = core == 0
    return jnp.concatenate(
        [jnp.where(lower, mine, theirs), jnp.where(lower, theirs, mine)], axis=0
    )


def solution(mesh):
    n_pix, n_tm = mesh.shape["pix"], mesh.shape["tm"]

    def local(frames, dark, dark_index, cycle_counts):
        owned, slots = frames.shape[1] // n_pix, frames.shape[2]
        fits = n_tm == 2 and owned == 2 * ROWS and n_pix & (n_pix - 1) == 0 and 2 < n_pix <= 8
        fits = fits and slots % (2 * LANES) == 0 and slots // 2 // LANES * ROWS % LANES == 0
        fits = fits and 4 * frames.shape[0] * n_pix <= LANES
        fits = fits and frames.shape[0] % 2 == 0 and dark.shape[0] % 2 == 0 and dark.shape[2] % LANES == 0 and slots == dark.shape[2] * n_pix
        return (packed_local if fits else plain_local)(frames, dark, dark_index, cycle_counts)

    in_specs = (
        P(("parts", "tm", "pix"), None, None),
        P("parts", None, "pix"),
        P(("parts", "tm")),
        P(),
    )
    out_specs = P("pix", ("parts", "tm"), None)
    return jax.shard_map(local, mesh=mesh, in_specs=in_specs, out_specs=out_specs, check_vma=False)
```

```python
import functools

import jax
import jax.numpy as jnp
from jax import lax
from jax.experimental import pallas as pl
from jax.experimental.pallas import tpu as pltpu
from jax.sharding import PartitionSpec as P

LANES = 128
ROWS = 16
FIRST = 2
ROOMS = (9, 10, 11, 12, 13)
VMEM_LIMIT = 16 * 1024 * 1024


def subtract_dark(raw_frames, dark_frames, dark_index, live_slot):
    values = raw_frames.astype(jnp.float32)
    for dark_level in range(dark_frames.shape[0]):
        picked = (dark_index == dark_level)[:, None, None]
        values = values - jnp.where(
            picked, dark_frames[dark_level].astype(jnp.float32)[None], jnp.float32(0.0)
        )
    return jnp.where(live_slot[None], values, jnp.float32(0.0)).astype(jnp.bfloat16)


def correlate(row_signal, col_signal):
    gram_tiles = jnp.einsum(
        "tqs,uqs->qtu", row_signal, col_signal, preferred_element_type=jnp.float32
    )
    totals = jnp.sum(col_signal, axis=2, dtype=jnp.float32).T
    return (gram_tiles, totals)


def plain_local(frames, dark, dark_index, cycle_counts):
    pix_count = lax.axis_size("pix")
    pix_index = lax.axis_index("pix")
    tm_index = lax.axis_index("tm")
    owned_cycles = frames.shape[1] // pix_count
    regrouped = lax.all_to_all(frames, "pix", split_axis=1, concat_axis=0, tiled=True)
    dark_cycles = lax.all_to_all(dark, "pix", split_axis=1, concat_axis=2, tiled=True)
    block_counts = lax.dynamic_slice_in_dim(cycle_counts, pix_index * owned_cycles, owned_cycles, 0)
    live_slot = jnp.arange(regrouped.shape[2], dtype=jnp.int32)[None, :] < block_counts[:, None]
    signal = subtract_dark(regrouped, dark_cycles, dark_index, live_slot)
    half_frames = signal.shape[0]
    all_frames = lax.all_gather(signal, "tm", axis=0, tiled=True)
    gram_tiles, totals = correlate(signal, all_frames)
    live_counts = lax.dynamic_slice_in_dim(
        cycle_counts, pix_index * owned_cycles, owned_cycles, 0
    ).astype(jnp.float32)
    row_totals = lax.dynamic_slice_in_dim(totals, tm_index * half_frames, half_frames, 1)
    return gram_tiles * live_counts[:, None, None] / (row_totals[:, :, None] * totals[:, None, :])


def plan_kernel(rooms, slots, counts, position, branch):
    receivers, units = position.shape
    every = (jnp.maximum(counts[...] - slots // 2, 0) + LANES - 1) // LANES
    own = (
        lax.broadcasted_iota(jnp.int32, (receivers, every.shape[1]), 1) // ROWS
        == lax.broadcasted_iota(jnp.int32, (receivers, every.shape[1]), 0)
    )
    repeat = (
        lax.broadcasted_iota(jnp.int32, (every.shape[1], units), 0) % ROWS
        == lax.broadcasted_iota(jnp.int32, (every.shape[1], units), 1) % ROWS
    )
    number = jnp.dot(
        jnp.where(own, every, 0).astype(jnp.float32).astype(jnp.bfloat16),
        jnp.where(repeat, 1.0, 0.0).astype(jnp.bfloat16),
        preferred_element_type=jnp.float32,
    )
    tile = lax.broadcasted_iota(jnp.int32, (receivers, units), 1) // ROWS
    live = tile.astype(jnp.float32) < number
    flags = jnp.where(live, 1.0, 0.0)
    before = (
        lax.broadcasted_iota(jnp.int32, (units, units), 0)
        < lax.broadcasted_iota(jnp.int32, (units, units), 1)
    )
    place = jnp.dot(
        flags.astype(jnp.bfloat16),
        jnp.where(before, 1.0, 0.0).astype(jnp.bfloat16),
        preferred_element_type=jnp.float32,
    )
    position[...] = jnp.where(live, place, -1.0)
    most = jnp.max(jnp.sum(flags, axis=1, keepdims=True)).astype(jnp.int32)
    branch[0] = sum(jnp.where(most > room, 1, 0) for room in rooms[:-1])


def chooser(position, receiver, room):
    units = position.shape[1]
    row = lax.broadcasted_iota(jnp.int32, (room, units), 0).astype(jnp.float32)
    return jnp.where(row == position[pl.ds(receiver, 1), :], 1.0, 0.0)


def pack_kernel(n_pix, room, messages, after, place, position, frames, dark, *refs):
    count = len(messages)
    refs = refs[after:]
    outs, (raw, shade, raw_sem, shade_sem) = refs[:count], refs[count:]
    per_device, slots = frames.shape[0], frames.shape[-1]
    share = shade.shape[1]
    lower = slots // 2 // LANES
    units = lower * ROWS
    copies = []
    for n, k in enumerate(messages):
        dest, half = place[0] ^ (k % n_pix), place[1] ^ (k // n_pix)
        copies.append((
            pltpu.make_async_copy(frames.at[:, dest, half], raw.at[n], raw_sem.at[n]),
            pltpu.make_async_copy(
                dark.at[pl.ds(place[1] * share, share), dest, half], shade.at[n], shade_sem.at[n]
            ),
        ))
        for copy in copies[-1]:
            copy.start()
    for n, k in enumerate(messages):
        for copy in copies[n]:
            copy.wait()
        row = 0
        for block, depth, tiles in (
            (raw, per_device, range(lower)),
            (shade, share, range(shade.shape[-1] // LANES)),
            (raw, per_device, range(lower, 2 * lower) if room == units else ()),
        ):
            for f in range(depth):
                for j in tiles:
                    outs[n][pl.ds(row, ROWS), :] = block[n, f, :, pl.ds(j * LANES, LANES)]
                    row += ROWS
        if room < units:
            dest, half = place[0] ^ (k % n_pix), place[1] ^ (k // n_pix)
            chosen = chooser(position, dest * 2 + half, room).astype(jnp.bfloat16)
            upper = jnp.concatenate(
                [
                    jnp.concatenate(
                        [raw[n, f, :, pl.ds(j * LANES, LANES)] for j in range(lower, 2 * lower)], axis=0
                    )
                    for f in range(per_device)
                ],
                axis=1,
            )
            live = jnp.dot(chosen, upper, preferred_element_type=jnp.float32)
            live = jnp.concatenate(
                [live[:, f * LANES : (f + 1) * LANES] for f in range(per_device)], axis=0
            )
            outs[n][pl.ds(row, per_device * room), :] = live.astype(jnp.bfloat16)


def split2(x):
    high = x.astype(jnp.bfloat16)
    rest = x - high.astype(jnp.float32)
    middle = rest.astype(jnp.bfloat16)
    return high, middle


def pick(x, chosen):
    return sum(jnp.dot(part, chosen, preferred_element_type=jnp.float32) for part in split2(x))


def gram_kernel(
    n_pix, per_device, levels, room, order, place, own_index, other_index, cycle_counts, position, *refs
):
    n_bufs = 2 * n_pix
    bufs, (mine, theirs, signal, dark) = dict(zip(order, refs)), refs[n_bufs:]
    me, core = place[0], place[1]
    share = levels // 2
    frames_half = per_device * n_pix
    n_frames = 2 * frames_half
    slots = signal.shape[1]
    tiles = slots // LANES
    dark_tiles = tiles // n_pix
    lower = tiles // 2
    units = lower * ROWS
    dark_row = per_device * units
    upper_row = dark_row + share * dark_tiles * ROWS
    if room < units:
        chosen = chooser(position, me * 2 + core, units).T.astype(jnp.bfloat16)[:, :room]
    lane = lax.broadcasted_iota(jnp.int32, (ROWS, LANES), 1)
    cycle = lax.broadcasted_iota(jnp.int32, (ROWS, LANES), 0)
    counts = jnp.zeros((ROWS, LANES), jnp.int32)
    for q in range(ROWS):
        count = cycle_counts[(2 * me + core) * ROWS + q]
        counts = jnp.where(cycle == q, count, counts)
    live = [lane + j * LANES < counts for j in range(tiles)]
    for k in range(n_bufs):
        source, half = me ^ (k % n_pix), core ^ (k // n_pix)
        for j in range(dark_tiles):
            for n in range(share):
                level = pl.multiple_of((half * share + n) * ROWS, ROWS)
                row = dark_row + (n * dark_tiles + j) * ROWS
                dark[source * dark_tiles + j, pl.ds(level, ROWS), :] = bufs[k][
                    pl.ds(row, ROWS), :
                ].astype(jnp.float32)
    for k in range(n_bufs):
        source, half = me ^ (k % n_pix), core ^ (k // n_pix)
        index = own_index if k < n_pix else other_index
        if room < units:
            packed = bufs[k][pl.ds(upper_row, per_device * room), :].astype(jnp.float32)
            packed = [packed[f * room : (f + 1) * room] for f in range(per_device)]
            upper = jnp.dot(
                chosen,
                jnp.concatenate(packed, axis=1).astype(jnp.bfloat16),
                preferred_element_type=jnp.float32,
            )
        for f in range(per_device):
            frame = source * per_device + f
            first = pl.multiple_of(((k // n_pix) * frames_half + frame) * ROWS, ROWS)
            dark_first = pl.multiple_of(index[frame] * ROWS, ROWS)
            for j in range(tiles):
                unit = (j % lower) * ROWS
                if j < lower:
                    raw = bufs[k][pl.ds(f * units + unit, ROWS), :].astype(jnp.float32)
                elif room < units:
                    raw = upper[unit : unit + ROWS, f * LANES : (f + 1) * LANES]
                else:
                    raw = bufs[k][pl.ds(upper_row + f * units + unit, ROWS), :].astype(jnp.float32)
                value = raw - dark[j, pl.ds(dark_first, ROWS), :]
                value = jnp.where(live[j], value, 0.0)
                signal[pl.ds(first, ROWS), pl.ds(j * LANES, LANES)] = value.astype(jnp.bfloat16)
    contract = (((1,), (1,)), ((), ()))
    width = n_frames * ROWS
    every = signal[...]
    totals = lax.dot_general(
        jnp.ones((ROWS, slots), jnp.bfloat16), every, contract, preferred_element_type=jnp.float32
    )
    products = lax.dot_general(every, every, contract, preferred_element_type=jnp.float32)
    products = jnp.concatenate([products, totals], axis=0)
    same = (
        lax.broadcasted_iota(jnp.int32, (ROWS, width), 0)
        == lax.broadcasted_iota(jnp.int32, (ROWS, width), 1) % ROWS
    )
    products = jnp.where(same[None], products.reshape(-1, ROWS, width), 0.0).reshape(-1, width)
    frame = lax.broadcasted_iota(jnp.int32, (width, LANES), 0) // ROWS
    lane = lax.broadcasted_iota(jnp.int32, (width, LANES), 1)
    place_out = (frame + core * frames_half) % n_frames
    fold = jnp.where((lane == place_out) | (lane == frame + n_frames), 1.0, 0.0)
    folded = pick(products, fold.astype(jnp.bfloat16))
    totals = folded[width:]
    counts = counts.astype(jnp.float32)[:, :n_frames]
    for t in range(n_frames):
        scale = totals[:, n_frames + t : n_frames + t + 1] * totals[:, :n_frames]
        block = folded[t * ROWS : (t + 1) * ROWS, :n_frames] * counts / scale
        out = mine if t < frames_half else theirs
        out[:, t % frames_half, :] = block


def in_vmem(count):
    return [pl.BlockSpec(memory_space=pltpu.VMEM)] * count


def in_smem(count):
    return [pl.BlockSpec(memory_space=pltpu.SMEM)] * count


def packed_local(frames, dark, dark_index, cycle_counts):
    n_pix, core, me = lax.axis_size("pix"), lax.axis_index("tm"), lax.axis_index("pix")
    per_device, _, slots = frames.shape
    levels, _, dark_slots = dark.shape
    n_frames = 2 * per_device * n_pix
    share = levels // 2
    units = slots // 2 // LANES * ROWS
    rooms = [units * part // 16 for part in ROOMS] + [units]
    swap = [(0, 1), (1, 0)]
    half = n_pix // 2
    far = [t * n_pix + k for t in range(2) for k in [*range(half, n_pix, 2), *range(half + 1, n_pix, 2)]]
    near = [t * n_pix + k for t in range(2) for k in range(1, half)] + [n_pix]
    order = far[:1] + [k for pair in zip(far[1:], near) for k in pair]
    messages = order + [0]
    count = len(messages)

    def exchange(room, place, position, frames, dark, own_index, cycle_counts):
        rows = per_device * (units + room) + share * dark_slots // LANES * ROWS
        packed = []
        for group in (messages[:FIRST], messages[FIRST:]):
            size, after = len(group), packed[:1]
            packed += pl.pallas_call(
                functools.partial(pack_kernel, n_pix, room, group, len(after)),
                out_shape=[jax.ShapeDtypeStruct((rows, LANES), frames.dtype)] * size,
                in_specs=in_smem(1) + in_vmem(1)
                + [pl.BlockSpec(memory_space=pltpu.HBM)] * 2
                + [pl.BlockSpec(memory_space=pl.ANY)] * len(after),
                out_specs=in_vmem(size),
                scratch_shapes=[
                    pltpu.VMEM((size, per_device, ROWS, slots), frames.dtype),
                    pltpu.VMEM((size, share, ROWS, dark_slots), dark.dtype),
                    pltpu.SemaphoreType.DMA((size,)),
                    pltpu.SemaphoreType.DMA((size,)),
                ],
                compiler_params=pltpu.CompilerParams(vmem_limit_bytes=VMEM_LIMIT),
                name="pack",
            )(
                place,
                position,
                pltpu.with_memory_space_constraint(frames, pltpu.HBM),
                pltpu.with_memory_space_constraint(dark, pltpu.HBM),
                *after,
            )
        other_index = lax.ppermute(own_index, "tm", swap)
        received = [
            lax.ppermute(buffer, ("tm", "pix"), [(i, i ^ k) for i in range(count)]) if k else buffer
            for k, buffer in zip(messages, packed)
        ]
        blocks = jax.ShapeDtypeStruct((ROWS, n_frames // 2, n_frames), jnp.float32)
        mine, send = pl.pallas_call(
            functools.partial(gram_kernel, n_pix, per_device, levels, room, messages),
            out_shape=[blocks, blocks],
            in_specs=in_smem(4) + in_vmem(1 + count),
            out_specs=in_vmem(2),
            scratch_shapes=[
                pltpu.VMEM((n_frames * ROWS, slots), jnp.bfloat16),
                pltpu.VMEM((slots // LANES, levels * ROWS, LANES), jnp.float32),
            ],
            compiler_params=pltpu.CompilerParams(vmem_limit_bytes=VMEM_LIMIT),
            name="gram",
        )(place, own_index, other_index, cycle_counts, position, *received)
        return mine, send

    place = jnp.stack([me, core]).astype(jnp.int32)
    position, branch = pl.pallas_call(
        functools.partial(plan_kernel, rooms, slots),
        out_shape=[
            jax.ShapeDtypeStruct((2 * n_pix, units), jnp.float32),
            jax.ShapeDtypeStruct((1,), jnp.int32),
        ],
        in_specs=in_vmem(1),
        out_specs=in_vmem(1) + in_smem(1),
        name="plan",
    )(cycle_counts.reshape(1, -1))
    mine, send = lax.switch(
        branch[0],
        [functools.partial(exchange, room) for room in rooms],
        place,
        position,
        frames.reshape(per_device, n_pix, 2, ROWS, slots),
        dark.reshape(levels, n_pix, 2, ROWS, dark_slots),
        dark_index,
        cycle_counts,
    )
    theirs = lax.ppermute(send, "tm", swap)
    lower = core == 0
    return jnp.concatenate(
        [jnp.where(lower, mine, theirs), jnp.where(lower, theirs, mine)], axis=0
    )


def solution(mesh):
    n_pix, n_tm = mesh.shape["pix"], mesh.shape["tm"]

    def local(frames, dark, dark_index, cycle_counts):
        owned, slots = frames.shape[1] // n_pix, frames.shape[2]
        fits = n_tm == 2 and owned == 2 * ROWS and n_pix & (n_pix - 1) == 0 and 2 < n_pix <= 8
        fits = fits and slots % (2 * LANES) == 0 and slots // 2 // LANES * ROWS % LANES == 0
        fits = fits and 4 * frames.shape[0] * n_pix <= LANES
        fits = fits and frames.shape[0] % 2 == 0 and dark.shape[0] % 2 == 0 and dark.shape[2] % LANES == 0 and slots == dark.shape[2] * n_pix
        return (packed_local if fits else plain_local)(frames, dark, dark_index, cycle_counts)

    in_specs = (
        P(("parts", "tm", "pix"), None, None),
        P("parts", None, "pix"),
        P(("parts", "tm")),
        P(),
    )
    out_specs = P("pix", ("parts", "tm"), None)
    return jax.shard_map(local, mesh=mesh, in_specs=in_specs, out_specs=out_specs, check_vma=False)
```
